256 devices in a mesh: vol: 32 (over x, z), view: 8 (over y, core).
Axes of the slice: x: 4, y: 4, z: 8, core: 2. Of those that a mesh axis runs over, the one named last changes fastest.
Arguments:
- volume: float32 [16, 32768], P(None, 'vol'), may hold values from -6 to 6
- row_footprint: float32 [64, 32, 80, 16], P('view', 'vol'), may hold values from 0 to 2.4, as said below
- column_footprint_weights: bfloat16 [32768, 3072], P('vol'), may hold values from 0 to 0.5, as said below
- tile_rows: int32 [32], P('vol'), may hold values from 0 to 16
- table_offset: int32 [64], P('view'), may hold values from 0 to 31
- view_angle: int32 [64], P('view'), may hold values from 0 to 3071
- measured: float32 [128, 64, 3072], P('vol', 'view'), may hold values from -6 to 6
- row_scale: float32 [128, 64, 3072], P('vol', 'view'), may hold values from 0.1 to 1
- column_scale: float32 [16, 32768], P(None, 'vol'), may hold values from 0.01 to 0.1
Outputs:
- updated: float32 [16, 32768], P(None, 'vol')
- weighted: float32 [128, 64, 3072], P('vol', 'view')
The draws below stay inside these ranges and needn't reach their ends.
Inputs may be any that keep to these rules, and one draw needn't show every extreme that they name: `row_footprint`: nonnegative banded weights. `column_footprint_weights`: nonnegative banded weights.
All inputs are finite; a program needn't handle non-finite values.
Results may differ from the reference program's by a relative error of at most 0.0026.
Values may be sent and summed in bfloat16 or wider, within the bound.
A program may use at most 128 MiB of HBM per device.

```python
import math
import jax
import jax.numpy as jnp
from jax import lax

S = 16
DC = 3072
DR = 128
FR = 80
ZSPAN = 32
VOX_DEV = 1024
NTILE = 32
NVOX = 32768
VIEWS = 64


def draw_row_footprint(key, part):
    key = jax.random.fold_in(key, 1)
    key_one, key_two = jax.random.split(key)
    row_index = jnp.arange(FR, dtype=jnp.float32)[:, None]
    slice_index = jnp.arange(S, dtype=jnp.float32)[None, :]
    jitter = jax.random.uniform(key_one, (VIEWS, NTILE, 1, S), jnp.float32, 0.0, 2.0)
    spacing = (FR - 3.0) / S
    stretch = max(1.0, spacing / 2.0)
    midpoint_value = slice_index * spacing + 1.0 + jitter
    distance = jnp.abs(row_index - midpoint_value) / stretch
    scales = jax.random.uniform(key_two, (VIEWS, NTILE, FR, S), jnp.float32, 0.5, 1.5)
    return scales * jnp.maximum(0.0, 1.6 - distance)


def draw_column_footprint_weights(key, part):
    key = jax.random.fold_in(key, 2)
    key_one, key_two = jax.random.split(key)
    start_positions = jax.random.randint(key_one, (NTILE,), 0, DC)
    voxel_position_index = jnp.arange(NVOX, dtype=jnp.int32)
    midpoint_value = voxel_position_index % VOX_DEV * DC // VOX_DEV + start_positions[voxel_position_index // VOX_DEV]
    column_index = jnp.arange(DC, dtype=jnp.int32)[None, :]
    distance = ((column_index - midpoint_value[:, None] + DC // 2) % DC - DC // 2).astype(jnp.float32)
    scales = jax.random.uniform(key_two, (NVOX, DC), jnp.float32, 0.5, 1.0)
    return (scales * jnp.maximum(0.0, 4.0 - jnp.abs(distance)) * 0.125).astype(jnp.bfloat16)


def set_ends(values, stream_key, low, high):
    dims = values.shape
    spot = [jax.random.randint(jax.random.fold_in(stream_key, axis), (), 0, dims[axis]) for axis in range(len(dims))]
    values = values.at[tuple(spot)].set(low)
    longest = dims.index(max(dims))
    spot[longest] = (spot[longest] + 1) % dims[longest]
    return values.at[tuple(spot)].set(high)


def shard_levels(own_key, extent, pieces, smallest, top_value):
    gain, own = 1.0, jax.random.fold_in(own_key, 6)
    for dim, shards_of in pieces:
        heights = jnp.exp(jax.random.uniform(jax.random.fold_in(own, dim), (shards_of,), jnp.float32, smallest / len(pieces), top_value / len(pieces)))
        gain = gain * jnp.repeat(heights, extent[dim] // shards_of).reshape([-1 if axis == dim else 1 for axis in range(len(extent))])
    return gain


def normal_values(key, extent, spread, limit, shards=(), kind=jnp.bfloat16):
    entries = jax.random.normal(key, extent, jnp.float32) * spread
    if len(shards) > 0:
        entries = shard_levels(key, extent, shards, -0.22, 0.18) * entries
    return jnp.clip(entries, min=-limit, max=limit).astype(kind)


def setup_inputs(seed: int = 0) -> dict:
    streams_of = jax.random.split(jax.random.key(seed), 10)
    return {
        "volume": normal_values(streams_of[0], (S, NVOX), 1.0, 6.0, ((1, 32),), jnp.float32),
        "row_footprint": draw_row_footprint(jax.random.fold_in(streams_of[9], 71), 0),
        "column_footprint_weights": draw_column_footprint_weights(jax.random.fold_in(streams_of[9], 71), 0),
        "tile_rows": set_ends(jax.random.randint(streams_of[3], (NTILE,), 0, DR - FR - ZSPAN + 1), jax.random.fold_in(streams_of[3], 1), 0, DR - FR - ZSPAN).astype(jnp.int32),
        "table_offset": set_ends(jax.random.randint(streams_of[4], (VIEWS,), 0, ZSPAN), jax.random.fold_in(streams_of[4], 1), 0, ZSPAN - 1).astype(jnp.int32),
        "view_angle": set_ends(jax.random.randint(streams_of[5], (VIEWS,), 0, DC), jax.random.fold_in(streams_of[5], 1), 0, DC - 1).astype(jnp.int32),
        "measured": normal_values(streams_of[6], (DR, VIEWS, DC), 1.0, 6.0, ((0, 32), (1, 8)), jnp.float32),
        "row_scale": jnp.clip(jnp.exp(math.log(1.0) - 2.3025851 * jax.random.uniform(streams_of[7], (DR, VIEWS, DC), jnp.float32) ** shard_levels(streams_of[7], (DR, VIEWS, DC), ((0, 32), (1, 8)), -0.2, 0.2)), 0.1, 1.0),
        "column_scale": jnp.clip(jnp.exp(math.log(0.1) - 2.3025851 * jax.random.uniform(streams_of[8], (S, NVOX), jnp.float32) ** shard_levels(streams_of[8], (S, NVOX), ((1, 32),), -0.2, 0.2)), 0.01, 0.1),
    }


def reference(volume, row_footprint, column_footprint_weights, tile_rows, table_offset, view_angle, measured, row_scale, column_scale):
    tile_count = tile_rows.shape[0]
    tile_data = volume.reshape(S, tile_count, VOX_DEV).transpose(1, 0, 2)
    column_tiles = column_footprint_weights.reshape(tile_count, VOX_DEV, DC)

    def view_step(back_sum, view_index):
        view_row_count = row_footprint[view_index]
        starts = tile_rows + table_offset[view_index]
        angle_now = view_angle[view_index]

        def forward_tile(tile_index, canvas):
            row_proj = jnp.dot(view_row_count[tile_index], tile_data[tile_index], precision=lax.Precision.HIGHEST).astype(jnp.bfloat16)
            block_data = jnp.roll(jnp.dot(row_proj, column_tiles[tile_index], preferred_element_type=jnp.float32), angle_now, axis=1)
            present_estimate = lax.dynamic_slice_in_dim(canvas, starts[tile_index], FR, 0)
            return lax.dynamic_update_slice_in_dim(canvas, present_estimate + block_data, starts[tile_index], 0)

        projection = lax.fori_loop(0, tile_count, forward_tile, jnp.zeros((DR, DC), jnp.float32))
        weighted = row_scale[:, view_index, :] * (measured[:, view_index, :] - projection)
        sent_rows = weighted.astype(jnp.bfloat16)

        def backward_tile(tile_index, back_now):
            window = jnp.roll(lax.dynamic_slice_in_dim(sent_rows, starts[tile_index], FR, 0), -angle_now, axis=1)
            back_cols = jnp.dot(window, column_tiles[tile_index].T, preferred_element_type=jnp.float32)
            contribution = jnp.dot(view_row_count[tile_index].T, back_cols, precision=lax.Precision.HIGHEST)
            return lax.dynamic_update_index_in_dim(back_now, back_now[tile_index] + contribution, tile_index, 0)

        back_sum = lax.fori_loop(0, tile_count, backward_tile, back_sum)
        return back_sum, weighted

    back_sum, weighted = lax.scan(view_step, jnp.zeros((tile_count, S, VOX_DEV), jnp.float32), jnp.arange(VIEWS, dtype=jnp.int32))
    updated = volume + column_scale * back_sum.transpose(1, 0, 2).reshape(S, tile_count * VOX_DEV)
    return updated, weighted.transpose(1, 0, 2)
```

```python
import functools

import jax
import jax.numpy as jnp
from jax import lax
from jax.experimental import pallas as pl
from jax.experimental.pallas import tpu as pltpu
from jax.sharding import PartitionSpec as P

MESH = pl.DeviceIdType.MESH
F32, BF16 = jnp.float32, jnp.bfloat16
S, FR, DR, DC, KV = 16, 80, 128, 3072, 1024
NX, NY, NZ, NV = 4, 4, 8, 8
CW = DC // 8
N_COPIES = 96


def split2(a):
    hi = a.astype(BF16)
    return hi, (a - hi.astype(F32)).astype(BF16)


def barrel(a, shift):
    for bit in range(12):
        moved = pltpu.roll(a, 1 << bit, 1)
        on = jnp.broadcast_to((shift >> bit) & 1, a.shape)
        a = jnp.where(on == 1, moved, a)
    return a


def kernel(
    vol_ref, foot_ref, key_ref, ang_ref, cs_ref, c_hbm, m_hbm, r_hbm,
    upd_ref, wtd_hbm,
    cbuf, mraw, rraw, ybuf, pbuf, gbuf, gt, a4, acat, atb,
    msend, rsend, mrecv, rrecv, wsend, wrecv, wout,
    zsend, zrecv, ssend, srecv, ubuf, ucore, uy, ufin, uother,
    lsem, ssem, rsem,
):
    d = lax.axis_index("vol")
    g = lax.axis_index("view")
    x, z = d // NZ, d % NZ
    y, c = g // 2, g % 2

    def xp(o):
        return (lax.rem(x + o, NX) * NZ + z, g)

    def zp(o):
        return (x * NZ + lax.rem(z + o, NZ), g)

    def vp(o):
        return (d, lax.rem(g + o, NV))

    def yp(o):
        return (d, lax.rem(y + o, NY) * 2 + c)

    core = (d, y * 2 + (1 - c))

    counter = [0]
    started = []

    def send(src, dst, device):
        n = counter[0]
        counter[0] += 1
        copy = pltpu.make_async_remote_copy(
            src_ref=src, dst_ref=dst, send_sem=ssem.at[n], recv_sem=rsem.at[n],
            device_id=device, device_id_type=MESH,
        )
        copy.start()
        started.append(copy)
        return copy

    barrier = pltpu.get_barrier_semaphore()
    partners = [xp(o) for o in range(1, NX)] + [zp(o) for o in range(1, NZ)] + [vp(o) for o in range(1, NV)]
    for device in partners:
        pl.semaphore_signal(barrier, inc=1, device_id=device, device_id_type=MESH)

    col0 = pl.multiple_of(g * CW, 128)
    c_in = pltpu.make_async_copy(c_hbm.at[:, pl.ds(col0, CW)], cbuf, lsem.at[0])
    m_in = pltpu.make_async_copy(m_hbm, mraw, lsem.at[1])
    r_in = pltpu.make_async_copy(r_hbm, rraw, lsem.at[2])
    c_in.start()
    m_in.start()
    r_in.start()

    f_hi, f_rest = split2(foot_ref[...])
    f_mid, f_lo = split2(foot_ref[...] - f_hi.astype(F32))
    f_all = jnp.concatenate([f_hi, f_mid, f_lo], axis=0)
    for zz in range(NZ):
        lane = lax.broadcasted_iota(jnp.int32, (128, 8 * FR), 0)
        row = (lane // 32) * 32 + zz * 4 + (lane % 32) // 8
        one_hot = (key_ref[...] == (lane % 8) * 1024 + row).astype(F32).astype(BF16)
        placed = lax.dot_general(f_all, one_hot, (((1,), (1,)), ((), ())), preferred_element_type=F32)
        pbuf[zz] = placed[:S] + placed[S : 2 * S] + placed[2 * S :]

    v_hi, v_lo = split2(vol_ref[...])
    c_in.wait()
    prod = jnp.dot(jnp.concatenate([v_hi, v_lo], axis=0), cbuf[...], preferred_element_type=F32)
    ybuf[d] = (prod[:S] + prod[S:]).astype(BF16)

    pl.semaphore_wait(barrier, len(partners))

    y_z = [send(ybuf.at[d], ybuf.at[d], zp(o)) for o in range(1, NZ)]
    f_z = [send(pbuf.at[lax.rem(z + o, NZ)], gbuf.at[z], zp(o)) for o in range(1, NZ)]
    y_x = [send(ybuf.at[d], ybuf.at[d], xp(o)) for o in range(1, NX)]
    gbuf[z] = pbuf[z]

    shift_back = jnp.where(ang_ref[...] == 0, 0, DC - ang_ref[...])
    exchanged = []
    for copy_in, raw, out, got in ((m_in, mraw, msend, mrecv), (r_in, rraw, rsend, rrecv)):
        copy_in.wait()
        for i in range(4):
            rolled = barrel(raw[8 * i : 8 * i + 8, :], shift_back)
            for k in range(NV):
                out[k, 8 * i : 8 * i + 8, :] = rolled[:, k * CW : (k + 1) * CW]
        for o in range(1, NV):
            exchanged.append(send(out.at[lax.rem(g + o, NV)], got.at[g], vp(o)))
        got[g] = out[g]

    for copy in f_z:
        copy.wait_recv()
    turned = jnp.transpose(gbuf[...].reshape(NZ * S, 128))
    gt[...] = turned.reshape(NX, 32, 128)
    f_x = [send(gt.at[lax.rem(x + o, NX)], a4.at[g, x], xp(o)) for o in range(1, NX)]
    a4[g, x] = gt[x]

    for o in range(1, NZ):
        y_z[o - 1].wait_recv()
        tile = x * NZ + lax.rem(z + NZ - o, NZ)
        y_x += [send(ybuf.at[tile], ybuf.at[tile], xp(p)) for p in range(1, NX)]

    for copy in f_x:
        copy.wait_recv()
    f_c = [send(a4.at[g], a4.at[g], core)]
    f_y = [send(a4.at[g], a4.at[g], yp(o)) for o in range(1, NY)]
    for o in range(1, NY):
        f_y[o - 1].wait_recv()
        group = lax.rem(y + NY - o, NY) * 2 + c
        f_c.append(send(a4.at[group], a4.at[group], core))
    for copy in f_c:
        copy.wait_recv()

    for k in range(NX):
        part = a4[:, k].reshape(NV * 32, 128)
        hi, lo = split2(part)
        acat[0:256, k * 128 : (k + 1) * 128] = hi
        acat[256:512, k * 128 : (k + 1) * 128] = lo
        t_hi, t_lo = split2(jnp.transpose(part))
        atb[k, :, 0:256] = t_hi
        atb[k, :, 256:512] = t_lo

    for copy in y_x:
        copy.wait_recv()
    proj = jnp.dot(acat[...], ybuf[...].reshape(NX * NZ * S, CW), preferred_element_type=F32)
    proj = proj[:256] + proj[256:]
    for copy in exchanged:
        copy.wait_recv()
    weighted = rrecv[...].reshape(256, CW) * (mrecv[...].reshape(256, CW) - proj)
    wsend[...] = weighted.reshape(NV, 32, CW)
    w_bf = weighted.astype(BF16)
    w_two = jnp.concatenate([w_bf, w_bf], axis=0)
    z_x = []
    for o in (1, 2, 3, 0):
        k = lax.rem(x + o, NX)
        part = jnp.dot(atb[k], w_two, preferred_element_type=F32)
        zsend[o] = part.astype(BF16)
        if o:
            z_x.append(send(zsend.at[o], zrecv.at[o - 1], xp(o)))

    w_v = [send(wsend.at[lax.rem(g + o, NV)], wrecv.at[g], vp(o)) for o in range(1, NV)]
    wrecv[g] = wsend[g]

    for copy in z_x:
        copy.wait_recv()
    total = zsend[0].astype(F32)
    for o in range(NX - 1):
        total += zrecv[o].astype(F32)
    ssend[...] = total.astype(BF16).reshape(NZ, S, CW)
    s_z = [send(ssend.at[lax.rem(z + o, NZ)], srecv.at[o - 1], zp(o)) for o in range(1, NZ)]

    for copy in w_v:
        copy.wait_recv()
    for i in range(4):
        row = jnp.concatenate([wrecv[k, 8 * i : 8 * i + 8, :] for k in range(NV)], axis=1)
        wout[8 * i : 8 * i + 8, :] = barrel(row, ang_ref[...])
    w_out = pltpu.make_async_copy(wout, wtd_hbm, lsem.at[3])
    w_out.start()

    for copy in s_z:
        copy.wait_recv()
    total = ssend[z].astype(F32)
    for o in range(NZ - 1):
        total += srecv[o].astype(F32)
    s_hi, s_lo = split2(total)
    back = lax.dot_general(
        jnp.concatenate([s_hi, s_lo], axis=0), cbuf[...], (((1,), (1,)), ((), ())), preferred_element_type=F32
    )
    back = back[:S] + back[S:]
    ubuf[0] = back[:, : KV // 2]
    ubuf[1] = back[:, KV // 2 :]
    u_c = send(ubuf.at[1 - c], ucore, core)
    u_c.wait_recv()
    uy[y] = ubuf[c] + ucore[...]
    u_y = [send(uy.at[y], uy.at[y], yp(o)) for o in range(1, NY)]
    for copy in u_y:
        copy.wait_recv()
    total = ((uy[0] + uy[1]) + uy[2]) + uy[3]
    half = pl.ds(pl.multiple_of(c * (KV // 2), 128), KV // 2)
    other = pl.ds(pl.multiple_of((1 - c) * (KV // 2), 128), KV // 2)
    ufin[...] = vol_ref[:, half] + cs_ref[:, half] * total
    u_f = send(ufin, uother, core)
    upd_ref[:, half] = ufin[...]
    u_f.wait_recv()
    upd_ref[:, other] = uother[...]
    for copy in started:
        copy.wait_send()
    w_out.wait()


def body(volume, row_footprint, column_footprint_weights, tile_rows, table_offset, view_angle, measured, row_scale, column_scale):
    starts = tile_rows[0] + table_offset
    key = (jnp.arange(8, dtype=jnp.int32)[:, None] * 1024 + starts[:, None] + jnp.arange(FR, dtype=jnp.int32)[None, :]).reshape(1, 8 * FR)
    foot = row_footprint[:, 0].reshape(8 * FR, S).T
    vmem = pl.BlockSpec(memory_space=pltpu.VMEM)
    hbm = pl.BlockSpec(memory_space=pl.ANY)
    updated, weighted = pl.pallas_call(
        kernel,
        out_shape=(jax.ShapeDtypeStruct((S, KV), F32), jax.ShapeDtypeStruct((32, DC), F32)),
        in_specs=[vmem] * 5 + [hbm] * 3,
        out_specs=(vmem, hbm),
        scratch_shapes=[
            pltpu.VMEM((KV, CW), BF16),
            pltpu.VMEM((32, DC), F32),
            pltpu.VMEM((32, DC), F32),
            pltpu.VMEM((32, S, CW), BF16),
            pltpu.VMEM((NZ, S, 128), F32),
            pltpu.VMEM((NZ, S, 128), F32),
            pltpu.VMEM((NX, 32, 128), F32),
            pltpu.VMEM((NV, NX, 32, 128), F32),
            pltpu.VMEM((512, 512), BF16),
            pltpu.VMEM((NX, 128, 512), BF16),
            pltpu.VMEM((NV, 32, CW), F32),
            pltpu.VMEM((NV, 32, CW), F32),
            pltpu.VMEM((NV, 32, CW), F32),
            pltpu.VMEM((NV, 32, CW), F32),
            pltpu.VMEM((NV, 32, CW), F32),
            pltpu.VMEM((NV, 32, CW), F32),
            pltpu.VMEM((32, DC), F32),
            pltpu.VMEM((NX, 128, CW), BF16),
            pltpu.VMEM((NX - 1, 128, CW), BF16),
            pltpu.VMEM((NZ, S, CW), BF16),
            pltpu.VMEM((NZ - 1, S, CW), BF16),
            pltpu.VMEM((2, S, KV // 2), F32),
            pltpu.VMEM((S, KV // 2), F32),
            pltpu.VMEM((NY, S, KV // 2), F32),
            pltpu.VMEM((S, KV // 2), F32),
            pltpu.VMEM((S, KV // 2), F32),
            pltpu.SemaphoreType.DMA((4,)),
            pltpu.SemaphoreType.DMA((N_COPIES,)),
            pltpu.SemaphoreType.DMA((N_COPIES,)),
        ],
        compiler_params=pltpu.CompilerParams(collective_id=0, has_side_effects=True, vmem_limit_bytes=40 << 20),
        cost_estimate=pl.CostEstimate(flops=500_000_000, bytes_accessed=3_000_000, transcendentals=0),
        name="sirt",
    )(
        volume, foot, key, view_angle.reshape(8, 1), column_scale, column_footprint_weights,
        measured.reshape(32, DC), row_scale.reshape(32, DC),
    )
    return updated, weighted.reshape(4, 8, DC)


def solution(mesh):
    placed = (
        P(None, "vol"),
        P("view", "vol", None, None),
        P("vol", None),
        P("vol"),
        P("view"),
        P("view"),
        P("vol", "view", None),
        P("vol", "view", None),
        P(None, "vol"),
    )
    return jax.shard_map(
        body,
        mesh=mesh,
        in_specs=placed,
        out_specs=(P(None, "vol"), P("vol", "view", None)),
        check_vma=False,
    )
```

```python
import functools

import jax
import jax.numpy as jnp
from jax import lax
from jax.experimental import pallas as pl
from jax.experimental.pallas import tpu as pltpu
from jax.sharding import PartitionSpec as P

MESH = pl.DeviceIdType.MESH
F32, BF16 = jnp.float32, jnp.bfloat16
S, FR, DR, DC, KV = 16, 80, 128, 3072, 1024
NX, NY, NZ, NV = 4, 4, 8, 8
CW = DC // 8
CHUNKS = ((0, 256), (256, 128))
N_COPIES = 160


def split2(a):
    hi = a.astype(BF16)
    return hi, (a - hi.astype(F32)).astype(BF16)


def barrel(a, shift):
    for bit in range(12):
        moved = pltpu.roll(a, 1 << bit, 1)
        on = jnp.broadcast_to((shift >> bit) & 1, a.shape)
        a = jnp.where(on == 1, moved, a)
    return a


def kernel(
    vol_hbm, foot_hbm, c_hbm, tile_hbm, offset_hbm, angle_hbm, m_hbm, r_hbm, cs_hbm,
    upd_hbm, wtd_hbm,
    vol_ref, foot_ref, cs_ref, tile_s, offset_s, angle_s, cbuf, cfull, mraw, rraw, ybuf, pbuf, gbuf, gt, a4, acat, atb,
    msend, rsend, mrecv, rrecv, psend, precv, wout,
    zsend0, zsend1, zrecv0, zrecv1, ssend0, ssend1, srecv0, srecv1, sall, ufin,
    lsem, ssem, rsem,
):
    d = lax.axis_index("vol")
    g = lax.axis_index("view")
    x, z = d // NZ, d % NZ
    y, c = g // 2, g % 2

    def xp(o):
        return (lax.rem(x + o, NX) * NZ + z, g)

    def zp(o):
        return (x * NZ + lax.rem(z + o, NZ), g)

    def vp(o):
        return (d, lax.rem(g + o, NV))

    def yp(o):
        return (d, lax.rem(y + o, NY) * 2 + c)

    def xyp(p, o):
        return (lax.rem(x + p, NX) * NZ + z, lax.rem(y + o, NY) * 2 + c)

    core = (d, y * 2 + (1 - c))

    counter = [0]
    started = []

    def send(src, dst, device):
        n = counter[0]
        counter[0] += 1
        copy = pltpu.make_async_remote_copy(
            src_ref=src, dst_ref=dst, send_sem=ssem.at[n], recv_sem=rsem.at[n],
            device_id=device, device_id_type=MESH,
        )
        copy.start()
        started.append(copy)
        return copy

    barrier = pltpu.get_barrier_semaphore()
    partners = [xp(o) for o in range(1, NX)] + [zp(o) for o in range(1, NZ)] + [vp(o) for o in range(1, NV)]
    partners += [xyp(p, o) for p in range(1, NX) for o in range(1, NY)]
    for device in partners:
        pl.semaphore_signal(barrier, inc=1, device_id=device, device_id_type=MESH)

    own_cols = pl.ds(pl.multiple_of(g * CW, 128), CW)
    fetches = [
        pltpu.make_async_copy(src, dst, lsem.at[n])
        for n, (src, dst) in enumerate((
            (tile_hbm, tile_s), (offset_hbm, offset_s), (angle_hbm, angle_s), (foot_hbm, foot_ref),
            (m_hbm, mraw), (r_hbm, rraw), (c_hbm.at[:, own_cols], cbuf), (vol_hbm, vol_ref),
            (cs_hbm, cs_ref), (c_hbm, cfull),
        ))
    ]
    for copy in fetches[:-1]:
        copy.start()
    tile_in, offset_in, angle_in, foot_in, m_in, r_in, c_in, vol_in, cs_in, cfull_in = fetches

    for copy in (tile_in, offset_in, angle_in, foot_in):
        copy.wait()
    view = lax.broadcasted_iota(jnp.int32, (8, 1), 0)
    start = jnp.zeros((8, 1), jnp.int32)
    angle = jnp.zeros((8, 1), jnp.int32)
    for v in range(8):
        start = jnp.where(view == v, tile_s[0] + offset_s[v], start)
        angle = jnp.where(view == v, angle_s[v], angle)
    foot = jnp.concatenate([jnp.pad(foot_ref[v], ((0, 0), (0, 128 - FR))) for v in range(8)], axis=1)
    f_all = jnp.concatenate(split2(foot), axis=0)
    source = lax.broadcasted_iota(jnp.int32, (128, 1024), 1)
    first = jnp.concatenate([start] * 16, axis=0)
    lane = lax.broadcasted_iota(jnp.int32, (128, 1), 0)
    for zz in range(NZ):
        wanted = (lane // 32) * 32 + zz * 4 + (lane % 32) // 8 - first
        wanted = jnp.where((wanted >= 0) & (wanted < FR), wanted + (lane % 8) * 128, -1)
        one_hot = (source == wanted).astype(F32).astype(BF16)
        placed = lax.dot_general(f_all, one_hot, (((1,), (1,)), ((), ())), preferred_element_type=F32)
        pbuf[zz] = placed[:S] + placed[S:]

    pl.semaphore_wait(barrier, len(partners))

    f_z = [send(pbuf.at[lax.rem(z + o, NZ)], gbuf.at[z], zp(o)) for o in range(1, NZ)]
    gbuf[z] = pbuf[z]

    shift_back = jnp.where(angle == 0, 0, DC - angle)
    exchanged = []
    for copy_in, raw, out, got in ((m_in, mraw, msend, mrecv), (r_in, rraw, rsend, rrecv)):
        copy_in.wait()
        for i in range(0, 4, 2):
            rolled = [barrel(raw[8 * n : 8 * n + 8, :], shift_back) for n in (i, i + 1)]
            rolled = jnp.concatenate(rolled, axis=0).astype(BF16)
            for k in range(NV):
                out[k, 8 * i : 8 * i + 16, :] = rolled[:, k * CW : (k + 1) * CW]
        for o in (4, 3, 5, 2, 6, 1, 7):
            exchanged.append(send(out.at[lax.rem(g + o, NV)], got.at[g], vp(o)))
        got[g] = out[g]

    vol_in.wait()
    v_all = jnp.concatenate(split2(vol_ref[...]), axis=0)
    c_in.wait()
    prod = jnp.dot(v_all, cbuf[...], preferred_element_type=F32)
    ybuf[d] = (prod[:S] + prod[S:]).astype(BF16)
    y_z = [send(ybuf.at[d], ybuf.at[d], zp(o)) for o in range(1, NZ)]
    y_x = [send(ybuf.at[d], ybuf.at[d], xp(o)) for o in range(1, NX)]
    cfull_in.start()

    for copy in f_z:
        copy.wait_recv()
    turned = jnp.transpose(gbuf[...].reshape(NZ * S, 128))
    gt[...] = turned.reshape(NX, 32, 128)
    f_xy = {}
    for p, o in [(p, o) for p in (0, 2, 1, 3) for o in (2, 1, 3, 0) if p or o]:
        f_xy[p, o] = send(gt.at[lax.rem(x + p, NX)], a4.at[g, x], xyp(p, o))
    a4[g, x] = gt[x]
    f_c = [send(gt.at[x], a4.at[g, x], core)]

    for o in range(1, NZ):
        y_z[o - 1].wait_recv()
        tile = x * NZ + lax.rem(z + NZ - o, NZ)
        y_x += [send(ybuf.at[tile], ybuf.at[tile], xp(p)) for p in range(1, NX)]

    for (p, o), copy in f_xy.items():
        copy.wait_recv()
        piece = a4.at[lax.rem(y + NY - o, NY) * 2 + c, lax.rem(x + NX - p, NX)]
        f_c.append(send(piece, piece, core))
    for copy in f_c:
        copy.wait_recv()

    for k in range(NX):
        part = a4[:, k].reshape(NV * 32, 128)
        hi, lo = split2(part)
        acat[0:256, k * 128 : (k + 1) * 128] = hi
        acat[256:512, k * 128 : (k + 1) * 128] = lo
        atb[k * 128 : (k + 1) * 128, :] = jnp.transpose(part).astype(BF16)

    for copy in y_x:
        copy.wait_recv()
    z_x = []
    for copy in exchanged:
        copy.wait_recv()
    for j, (first, width) in enumerate(CHUNKS):
        cols = pl.ds(first, width)
        zsend, zrecv = ((zsend0, zrecv0), (zsend1, zrecv1))[j]
        proj = jnp.dot(acat[...], ybuf[:, :, cols].reshape(NX * NZ * S, width), preferred_element_type=F32)
        proj = proj[:256] + proj[256:]
        psend[:, :, cols] = proj.reshape(NV, 32, width)
        measured = mrecv[:, :, cols].astype(F32).reshape(256, width)
        weighted = rrecv[:, :, cols].astype(F32).reshape(256, width) * (measured - proj)
        part = jnp.dot(atb[...], weighted.astype(BF16), preferred_element_type=F32)
        zsend[...] = part.astype(BF16).reshape(NX, 128, width)
        z_x.append([send(zsend.at[lax.rem(x + o, NX)], zrecv.at[o - 1], xp(o)) for o in (2, 1, 3)])

    p_v = [send(psend.at[lax.rem(g + o, NV)], precv.at[g], vp(o)) for o in (1, 7, 2, 6, 3, 5, 4)]
    precv[g] = psend[g]

    s_z = []
    for j, (first, width) in enumerate(CHUNKS):
        zsend, zrecv = ((zsend0, zrecv0), (zsend1, zrecv1))[j]
        ssend, srecv = ((ssend0, srecv0), (ssend1, srecv1))[j]
        for copy in z_x[j]:
            copy.wait_recv()
        total = zsend[x].astype(F32)
        for o in range(NX - 1):
            total += zrecv[o].astype(F32)
        ssend[...] = total.astype(BF16).reshape(NZ, S, width)
        s_z.append([send(ssend.at[lax.rem(z + o, NZ)], srecv.at[o - 1], zp(o)) for o in (4, 3, 5, 2, 6, 1, 7)])

    for j, (first, width) in enumerate(CHUNKS):
        ssend, srecv = ((ssend0, srecv0), (ssend1, srecv1))[j]
        for copy in s_z[j]:
            copy.wait_recv()
        total = ssend[z].astype(F32)
        for o in range(NZ - 1):
            total += srecv[o].astype(F32)
        sall[g, :, first : first + width] = total.astype(BF16)

    s_v = {o: send(sall.at[g], sall.at[g], vp(o)) for o in (4, 3, 5, 2, 6, 1, 7)}

    for copy in p_v:
        copy.wait_recv()
    for i in range(4):
        rows = slice(8 * i, 8 * i + 8)
        row = jnp.concatenate([precv[k, rows, :] for k in range(NV)], axis=1)
        wout[rows, :] = rraw[rows, :] * (mraw[rows, :] - barrel(row, angle))
    w_out = pltpu.make_async_copy(wout, wtd_hbm, lsem.at[10])
    w_out.start()

    cfull_in.wait()
    cs_in.wait()

    for copy in s_v.values():
        copy.wait_recv()
    both = jnp.concatenate([sall[k] for k in range(NV)], axis=1)
    total = lax.dot_general(both, cfull[...], (((1,), (1,)), ((), ())), preferred_element_type=F32)

    ufin[...] = vol_ref[...] + cs_ref[...] * total
    u_out = pltpu.make_async_copy(ufin, upd_hbm, lsem.at[11])
    u_out.start()
    for copy in started:
        copy.wait_send()
    w_out.wait()
    u_out.wait()


def hand_over(upd_in, wtd_in, upd_out, wtd_out, upd_held, wtd_held, sem):
    pieces = [(upd_in, upd_held, upd_out)] + [(wtd_in.at[i], wtd_held.at[i], wtd_out.at[i]) for i in range(4)]
    arriving = [pltpu.make_async_copy(src, held, sem.at[n]) for n, (src, held, _) in enumerate(pieces)]
    leaving = [pltpu.make_async_copy(held, dst, sem.at[5 + n]) for n, (_, held, dst) in enumerate(pieces)]
    for copy in arriving:
        copy.start()
    for n in range(5):
        arriving[n].wait()
        leaving[n].start()
    for copy in leaving:
        copy.wait()


def body(volume, row_footprint, column_footprint_weights, tile_rows, table_offset, view_angle, measured, row_scale, column_scale):
    foot = jnp.transpose(row_footprint[:, 0], (0, 2, 1))
    hbm = pl.BlockSpec(memory_space=pltpu.HBM)
    updated, weighted = pl.pallas_call(
        kernel,
        out_shape=(jax.ShapeDtypeStruct((S, KV), F32), jax.ShapeDtypeStruct((32, DC), F32)),
        in_specs=[hbm] * 9,
        out_specs=(hbm, hbm),
        scratch_shapes=[
            pltpu.VMEM((S, KV), F32),
            pltpu.VMEM((8, S, FR), F32),
            pltpu.VMEM((S, KV), F32),
            pltpu.SMEM((1,), jnp.int32),
            pltpu.SMEM((8,), jnp.int32),
            pltpu.SMEM((8,), jnp.int32),
            pltpu.VMEM((KV, CW), BF16),
            pltpu.VMEM((KV, DC), BF16),
            pltpu.VMEM((32, DC), F32),
            pltpu.VMEM((32, DC), F32),
            pltpu.VMEM((32, S, CW), BF16),
            pltpu.VMEM((NZ, S, 128), F32),
            pltpu.VMEM((NZ, S, 128), F32),
            pltpu.VMEM((NX, 32, 128), F32),
            pltpu.VMEM((NV, NX, 32, 128), F32),
            pltpu.VMEM((512, 512), BF16),
            pltpu.VMEM((512, 256), BF16),
            pltpu.VMEM((NV, 32, CW), BF16),
            pltpu.VMEM((NV, 32, CW), BF16),
            pltpu.VMEM((NV, 32, CW), BF16),
            pltpu.VMEM((NV, 32, CW), BF16),
            pltpu.VMEM((NV, 32, CW), F32),
            pltpu.VMEM((NV, 32, CW), F32),
            pltpu.VMEM((32, DC), F32),
            pltpu.VMEM((NX, 128, 256), BF16),
            pltpu.VMEM((NX, 128, 128), BF16),
            pltpu.VMEM((NX - 1, 128, 256), BF16),
            pltpu.VMEM((NX - 1, 128, 128), BF16),
            pltpu.VMEM((NZ, S, 256), BF16),
            pltpu.VMEM((NZ, S, 128), BF16),
            pltpu.VMEM((NZ - 1, S, 256), BF16),
            pltpu.VMEM((NZ - 1, S, 128), BF16),
            pltpu.VMEM((NV, S, CW), BF16),
            pltpu.VMEM((S, KV), F32),
            pltpu.SemaphoreType.DMA((12,)),
            pltpu.SemaphoreType.DMA((N_COPIES,)),
            pltpu.SemaphoreType.DMA((N_COPIES,)),
        ],
        compiler_params=pltpu.CompilerParams(collective_id=0, has_side_effects=True, vmem_limit_bytes=60 << 20),
        cost_estimate=pl.CostEstimate(flops=500_000_000, bytes_accessed=3_000_000, transcendentals=0),
        name="sirt",
    )(
        volume, foot, column_footprint_weights, tile_rows, table_offset, view_angle,
        measured.reshape(32, DC), row_scale.reshape(32, DC), column_scale,
    )
    return pl.pallas_call(
        hand_over,
        out_shape=(jax.ShapeDtypeStruct((S, KV), F32), jax.ShapeDtypeStruct((4, 8, DC), F32)),
        in_specs=[hbm] * 2,
        out_specs=(hbm, hbm),
        scratch_shapes=[pltpu.VMEM((S, KV), F32), pltpu.VMEM((4, 8, DC), F32), pltpu.SemaphoreType.DMA((10,))],
        compiler_params=pltpu.CompilerParams(vmem_limit_bytes=60 << 20),
        name="hand_over",
    )(updated, weighted.reshape(4, 8, DC))


def solution(mesh):
    placed = (
        P(None, "vol"),
        P("view", "vol", None, None),
        P("vol", None),
        P("vol"),
        P("view"),
        P("view"),
        P("vol", "view", None),
        P("vol", "view", None),
        P(None, "vol"),
    )
    return jax.shard_map(
        body,
        mesh=mesh,
        in_specs=placed,
        out_specs=(P(None, "vol"), P("vol", "view", None)),
        check_vma=False,
    )
```

```python
import functools

import jax
import jax.numpy as jnp
from jax import lax
from jax.experimental import pallas as pl
from jax.experimental.pallas import tpu as pltpu
from jax.sharding import PartitionSpec as P

MESH = pl.DeviceIdType.MESH
F32, BF16 = jnp.float32, jnp.bfloat16
S, FR, DR, DC, KV = 16, 80, 128, 3072, 1024
NX, NY, NZ, NV = 4, 4, 8, 8
CW = DC // 8
CHUNKS = ((0, 256), (256, 128))
N_COPIES = 160


def split2(a):
    hi = a.astype(BF16)
    return hi, (a - hi.astype(F32)).astype(BF16)


def barrel(a, shift):
    for bit in range(12):
        moved = pltpu.roll(a, 1 << bit, 1)
        on = jnp.broadcast_to((shift >> bit) & 1, a.shape)
        a = jnp.where(on == 1, moved, a)
    return a


def kernel(
    vol_hbm, foot_hbm, c_hbm, tile_hbm, offset_hbm, angle_hbm, m_hbm, r_hbm, cs_hbm,
    upd_hbm, wtd_hbm,
    vol_ref, foot_ref, cs_ref, tile_s, offset_s, angle_s, cbuf, cfull, mraw, rraw, ybuf, pbuf, gbuf, gt, a4, acat, atb,
    msend, rsend, mrecv, rrecv, psend, precv, wout,
    zsend0, zsend1, zrecv0, zrecv1, ssend0, ssend1, srecv0, srecv1, sall, uall, ufin,
    lsem, ssem, rsem,
):
    d = lax.axis_index("vol")
    g = lax.axis_index("view")
    x, z = d // NZ, d % NZ
    y, c = g // 2, g % 2

    def xp(o):
        return (lax.rem(x + o, NX) * NZ + z, g)

    def zp(o):
        return (x * NZ + lax.rem(z + o, NZ), g)

    def vp(o):
        return (d, lax.rem(g + o, NV))

    def yp(o):
        return (d, lax.rem(y + o, NY) * 2 + c)

    def vq(o, swap):
        return (d, lax.rem(y + o, NY) * 2 + (1 - c if swap else c))

    def xyp(p, o):
        return (lax.rem(x + p, NX) * NZ + z, lax.rem(y + o, NY) * 2 + c)

    core = (d, y * 2 + (1 - c))

    counter = [0]
    started = []

    def send(src, dst, device):
        n = counter[0]
        counter[0] += 1
        copy = pltpu.make_async_remote_copy(
            src_ref=src, dst_ref=dst, send_sem=ssem.at[n], recv_sem=rsem.at[n],
            device_id=device, device_id_type=MESH,
        )
        copy.start()
        started.append(copy)
        return copy

    barrier = pltpu.get_barrier_semaphore()
    partners = [xp(o) for o in range(1, NX)] + [zp(o) for o in range(1, NZ)] + [vp(o) for o in range(1, NV)]
    partners += [xyp(p, o) for p in range(1, NX) for o in range(1, NY)]
    for device in partners:
        pl.semaphore_signal(barrier, inc=1, device_id=device, device_id_type=MESH)

    own_cols = pl.ds(pl.multiple_of(g * CW, 128), CW)
    fetches = [
        pltpu.make_async_copy(src, dst, lsem.at[n])
        for n, (src, dst) in enumerate((
            (tile_hbm, tile_s), (offset_hbm, offset_s), (angle_hbm, angle_s), (foot_hbm, foot_ref),
            (m_hbm, mraw), (r_hbm, rraw), (c_hbm.at[:, own_cols], cbuf), (vol_hbm, vol_ref),
            (cs_hbm, cs_ref), (c_hbm, cfull),
        ))
    ]
    for copy in fetches[:-1]:
        copy.start()
    tile_in, offset_in, angle_in, foot_in, m_in, r_in, c_in, vol_in, cs_in, cfull_in = fetches

    for copy in (tile_in, offset_in, angle_in, foot_in):
        copy.wait()
    view = lax.broadcasted_iota(jnp.int32, (8, 1), 0)
    start = jnp.zeros((8, 1), jnp.int32)
    angle = jnp.zeros((8, 1), jnp.int32)
    for v in range(8):
        start = jnp.where(view == v, tile_s[0] + offset_s[v], start)
        angle = jnp.where(view == v, angle_s[v], angle)
    foot = jnp.concatenate([jnp.pad(foot_ref[v], ((0, 0), (0, 128 - FR))) for v in range(8)], axis=1)
    f_all = jnp.concatenate(split2(foot), axis=0)
    source = lax.broadcasted_iota(jnp.int32, (128, 1024), 1)
    first = jnp.concatenate([start] * 16, axis=0)
    lane = lax.broadcasted_iota(jnp.int32, (128, 1), 0)
    for zz in range(NZ):
        wanted = (lane // 32) * 32 + zz * 4 + (lane % 32) // 8 - first
        wanted = jnp.where((wanted >= 0) & (wanted < FR), wanted + (lane % 8) * 128, -1)
        one_hot = (source == wanted).astype(F32).astype(BF16)
        placed = lax.dot_general(f_all, one_hot, (((1,), (1,)), ((), ())), preferred_element_type=F32)
        pbuf[zz] = placed[:S] + placed[S:]

    pl.semaphore_wait(barrier, len(partners))

    f_z = [send(pbuf.at[lax.rem(z + o, NZ)], gbuf.at[z], zp(o)) for o in range(1, NZ)]
    gbuf[z] = pbuf[z]

    shift_back = jnp.where(angle == 0, 0, DC - angle)
    exchanged = []
    for copy_in, raw, out, got in ((m_in, mraw, msend, mrecv), (r_in, rraw, rsend, rrecv)):
        copy_in.wait()
        for i in range(0, 4, 2):
            rolled = [barrel(raw[8 * n : 8 * n + 8, :], shift_back) for n in (i, i + 1)]
            rolled = jnp.concatenate(rolled, axis=0).astype(BF16)
            for k in range(NV):
                out[k, 8 * i : 8 * i + 16, :] = rolled[:, k * CW : (k + 1) * CW]
        for o in (4, 3, 5, 2, 6, 1, 7):
            exchanged.append(send(out.at[lax.rem(g + o, NV)], got.at[g], vp(o)))
        got[g] = out[g]

    vol_in.wait()
    v_all = jnp.concatenate(split2(vol_ref[...]), axis=0)
    c_in.wait()
    prod = jnp.dot(v_all, cbuf[...], preferred_element_type=F32)
    ybuf[d] = (prod[:S] + prod[S:]).astype(BF16)
    y_z = [send(ybuf.at[d], ybuf.at[d], zp(o)) for o in range(1, NZ)]
    y_x = [send(ybuf.at[d], ybuf.at[d], xp(o)) for o in range(1, NX)]
    cfull_in.start()

    for copy in f_z:
        copy.wait_recv()
    turned = jnp.transpose(gbuf[...].reshape(NZ * S, 128))
    gt[...] = turned.reshape(NX, 32, 128)
    f_xy = {}
    for p, o in [(p, o) for p in (0, 2, 1, 3) for o in (2, 1, 3, 0) if p or o]:
        f_xy[p, o] = send(gt.at[lax.rem(x + p, NX)], a4.at[g, x], xyp(p, o))
    a4[g, x] = gt[x]
    f_c = [send(gt.at[x], a4.at[g, x], core)]

    for o in range(1, NZ):
        y_z[o - 1].wait_recv()
        tile = x * NZ + lax.rem(z + NZ - o, NZ)
        y_x += [send(ybuf.at[tile], ybuf.at[tile], xp(p)) for p in range(1, NX)]

    for (p, o), copy in f_xy.items():
        copy.wait_recv()
        piece = a4.at[lax.rem(y + NY - o, NY) * 2 + c, lax.rem(x + NX - p, NX)]
        f_c.append(send(piece, piece, core))
    for copy in f_c:
        copy.wait_recv()

    for k in range(NX):
        part = a4[:, k].reshape(NV * 32, 128)
        hi, lo = split2(part)
        acat[0:256, k * 128 : (k + 1) * 128] = hi
        acat[256:512, k * 128 : (k + 1) * 128] = lo
        atb[k * 128 : (k + 1) * 128, :] = jnp.transpose(part).astype(BF16)

    for copy in y_x:
        copy.wait_recv()
    for copy in exchanged:
        copy.wait_recv()
    for j, (first, width) in enumerate(CHUNKS):
        cols = pl.ds(first, width)
        proj = jnp.dot(acat[...], ybuf[:, :, cols].reshape(NX * NZ * S, width), preferred_element_type=F32)
        proj = proj[:256] + proj[256:]
        psend[:, :, cols] = proj.reshape(NV, 32, width)
        measured = mrecv[:, :, cols].astype(F32).reshape(256, width)
        weighted = rrecv[:, :, cols].astype(F32).reshape(256, width) * (measured - proj)
        part = jnp.dot(atb[...], weighted.astype(BF16), preferred_element_type=F32)
        part = part.astype(BF16)
        if j == 0:
            zsend0[...] = part.reshape(NX, 128, width)
            z0_x = [send(zsend0.at[lax.rem(x + o, NX)], zrecv0.at[o - 1], xp(o)) for o in (2, 1, 3)]
        else:
            zsend1[...] = part.reshape(NX, NZ, S, width)
            z1_z = [send(zsend1.at[:, lax.rem(z + o, NZ)], zrecv1.at[o - 1], zp(o)) for o in (4, 3, 5, 2, 6, 1, 7)]

    p_v = [send(psend.at[lax.rem(g + o, NV)], precv.at[g], vp(o)) for o in (1, 7, 2, 6, 3, 5, 4)]
    precv[g] = psend[g]

    for copy in z0_x:
        copy.wait_recv()
    total = zsend0[x].astype(F32)
    for o in range(NX - 1):
        total += zrecv0[o].astype(F32)
    ssend0[...] = total.astype(BF16).reshape(NZ, S, 256)
    z0_z = [send(ssend0.at[lax.rem(z + o, NZ)], srecv0.at[o - 1], zp(o)) for o in (4, 3, 5, 2, 6, 1, 7)]

    for copy in z1_z:
        copy.wait_recv()
    total = zsend1[:, z].astype(F32)
    for o in range(NZ - 1):
        total += zrecv1[o].astype(F32)
    ssend1[...] = total.astype(BF16)
    z1_x = [send(ssend1.at[lax.rem(x + o, NX)], srecv1.at[o - 1], xp(o)) for o in (2, 1, 3)]

    for copy in z0_z:
        copy.wait_recv()
    total = ssend0[z].astype(F32)
    for o in range(NZ - 1):
        total += srecv0[o].astype(F32)
    sall[g, :, :256] = total.astype(BF16)

    for copy in z1_x:
        copy.wait_recv()
    total = ssend1[x].astype(F32)
    for o in range(NX - 1):
        total += srecv1[o].astype(F32)
    sall[g, :, 256:] = total.astype(BF16)

    s_v = {o: [send(sall.at[g], sall.at[g], vq(o, swap)) for swap in (False, True)] for o in (2, 1, 3)}
    s_v[0] = send(sall.at[g], sall.at[g], core)

    for copy in p_v:
        copy.wait_recv()
    for i in range(4):
        rows = slice(8 * i, 8 * i + 8)
        row = jnp.concatenate([precv[k, rows, :] for k in range(NV)], axis=1)
        wout[rows, :] = rraw[rows, :] * (mraw[rows, :] - barrel(row, angle))
    w_out = pltpu.make_async_copy(wout, wtd_hbm, lsem.at[10])
    w_out.start()

    cfull_in.wait()
    cs_in.wait()
    for o in (0, 1, 3, 2):
        if not o:
            s_v[0].wait_recv()
        else:
            for copy in s_v[o]:
                copy.wait_recv()
        group = lax.rem(y + NY - o, NY)
        both = jnp.concatenate([sall[2 * group], sall[2 * group + 1]], axis=1)
        weights = cfull[:, pl.ds(pl.multiple_of(group * 2 * CW, 128), 2 * CW)]
        uall[group] = lax.dot_general(both, weights, (((1,), (1,)), ((), ())), preferred_element_type=F32)

    total = ((uall[0] + uall[1]) + uall[2]) + uall[3]
    ufin[...] = vol_ref[...] + cs_ref[...] * total
    u_out = pltpu.make_async_copy(ufin, upd_hbm, lsem.at[11])
    u_out.start()
    for copy in started:
        copy.wait_send()
    w_out.wait()
    u_out.wait()


def hand_over(upd_in, wtd_in, upd_out, wtd_out, upd_held, wtd_held, sem):
    pieces = [(upd_in, upd_held, upd_out)] + [(wtd_in.at[i], wtd_held.at[i], wtd_out.at[i]) for i in range(4)]
    arriving = [pltpu.make_async_copy(src, held, sem.at[n]) for n, (src, held, _) in enumerate(pieces)]
    leaving = [pltpu.make_async_copy(held, dst, sem.at[5 + n]) for n, (_, held, dst) in enumerate(pieces)]
    for copy in arriving:
        copy.start()
    for n in range(5):
        arriving[n].wait()
        leaving[n].start()
    for copy in leaving:
        copy.wait()


def body(volume, row_footprint, column_footprint_weights, tile_rows, table_offset, view_angle, measured, row_scale, column_scale):
    foot = jnp.transpose(row_footprint[:, 0], (0, 2, 1))
    hbm = pl.BlockSpec(memory_space=pltpu.HBM)
    updated, weighted = pl.pallas_call(
        kernel,
        out_shape=(jax.ShapeDtypeStruct((S, KV), F32), jax.ShapeDtypeStruct((32, DC), F32)),
        in_specs=[hbm] * 9,
        out_specs=(hbm, hbm),
        scratch_shapes=[
            pltpu.VMEM((S, KV), F32),
            pltpu.VMEM((8, S, FR), F32),
            pltpu.VMEM((S, KV), F32),
            pltpu.SMEM((1,), jnp.int32),
            pltpu.SMEM((8,), jnp.int32),
            pltpu.SMEM((8,), jnp.int32),
            pltpu.VMEM((KV, CW), BF16),
            pltpu.VMEM((KV, DC), BF16),
            pltpu.VMEM((32, DC), F32),
            pltpu.VMEM((32, DC), F32),
            pltpu.VMEM((32, S, CW), BF16),
            pltpu.VMEM((NZ, S, 128), F32),
            pltpu.VMEM((NZ, S, 128), F32),
            pltpu.VMEM((NX, 32, 128), F32),
            pltpu.VMEM((NV, NX, 32, 128), F32),
            pltpu.VMEM((512, 512), BF16),
            pltpu.VMEM((512, 256), BF16),
            pltpu.VMEM((NV, 32, CW), BF16),
            pltpu.VMEM((NV, 32, CW), BF16),
            pltpu.VMEM((NV, 32, CW), BF16),
            pltpu.VMEM((NV, 32, CW), BF16),
            pltpu.VMEM((NV, 32, CW), F32),
            pltpu.VMEM((NV, 32, CW), F32),
            pltpu.VMEM((32, DC), F32),
            pltpu.VMEM((NX, 128, 256), BF16),
            pltpu.VMEM((NX, NZ, S, 128), BF16),
            pltpu.VMEM((NX - 1, 128, 256), BF16),
            pltpu.VMEM((NZ - 1, NX, S, 128), BF16),
            pltpu.VMEM((NZ, S, 256), BF16),
            pltpu.VMEM((NX, S, 128), BF16),
            pltpu.VMEM((NZ - 1, S, 256), BF16),
            pltpu.VMEM((NX - 1, S, 128), BF16),
            pltpu.VMEM((NV, S, CW), BF16),
            pltpu.VMEM((NY, S, KV), F32),
            pltpu.VMEM((S, KV), F32),
            pltpu.SemaphoreType.DMA((12,)),
            pltpu.SemaphoreType.DMA((N_COPIES,)),
            pltpu.SemaphoreType.DMA((N_COPIES,)),
        ],
        compiler_params=pltpu.CompilerParams(collective_id=0, has_side_effects=True, vmem_limit_bytes=60 << 20),
        cost_estimate=pl.CostEstimate(flops=500_000_000, bytes_accessed=3_000_000, transcendentals=0),
        name="sirt",
    )(
        volume, foot, column_footprint_weights, tile_rows, table_offset, view_angle,
        measured.reshape(32, DC), row_scale.reshape(32, DC), column_scale,
    )
    return pl.pallas_call(
        hand_over,
        out_shape=(jax.ShapeDtypeStruct((S, KV), F32), jax.ShapeDtypeStruct((4, 8, DC), F32)),
        in_specs=[hbm] * 2,
        out_specs=(hbm, hbm),
        scratch_shapes=[pltpu.VMEM((S, KV), F32), pltpu.VMEM((4, 8, DC), F32), pltpu.SemaphoreType.DMA((10,))],
        compiler_params=pltpu.CompilerParams(vmem_limit_bytes=60 << 20),
        name="hand_over",
    )(updated, weighted.reshape(4, 8, DC))


def solution(mesh):
    placed = (
        P(None, "vol"),
        P("view", "vol", None, None),
        P("vol", None),
        P("vol"),
        P("view"),
        P("view"),
        P("vol", "view", None),
        P("vol", "view", None),
        P(None, "vol"),
    )
    return jax.shard_map(
        body,
        mesh=mesh,
        in_specs=placed,
        out_specs=(P(None, "vol"), P("vol", "view", None)),
        check_vma=False,
    )
```

```python
import functools

import jax
import jax.numpy as jnp
from jax import lax
from jax.experimental import pallas as pl
from jax.experimental.pallas import tpu as pltpu
from jax.sharding import PartitionSpec as P

MESH = pl.DeviceIdType.MESH
F32, BF16 = jnp.float32, jnp.bfloat16
S, FR, DR, DC, KV = 16, 80, 128, 3072, 1024
NX, NY, NZ, NV = 4, 4, 8, 8
CW = DC // 8
CHUNKS = ((0, 256), (256, 128))
FAR_Z = (4, 3, 5, 2, 6, 1, 7)
(FZ_S, M_S, R_S, Y1X_S, Y1Z_S, Y0Z_S, Y0X_S, F_S, _, FC_S, Z0X_S, Z1Z_S, Z0Z_S, Z1X_S, P_S, SV_S) = range(16)
(FZ_R, M_R, R_R, Y1Z_R, Y0X_R, FC_R, Z0X_R, Z1Z_R, Z0Z_R, Z1X_R, P_R) = range(11)
Y1X_R, Y0Z_R, F_R, SV_R = 11, 14, 21, 25
N_SENT, N_ARRIVED = 16, 29


def split2(a):
    hi = a.astype(BF16)
    return hi, (a - hi.astype(F32)).astype(BF16)


def barrel(a, shift):
    for bit in range(12):
        moved = pltpu.roll(a, 1 << bit, 1)
        on = jnp.broadcast_to((shift >> bit) & 1, a.shape)
        a = jnp.where(on == 1, moved, a)
    return a


def kernel(
    vol_hbm, foot_hbm, c_hbm, tile_hbm, offset_hbm, angle_hbm, m_hbm, r_hbm, cs_hbm,
    upd_hbm, wtd_hbm,
    vol_ref, foot_ref, cs_ref, tile_s, offset_s, angle_s, cbuf, cfull, mraw, rraw, ybuf0, ybuf1, pbuf, gbuf, gt, a4, acat, atb,
    msend, rsend, mrecv, rrecv, psend, precv, wout,
    zsend0, zsend1, zrecv0, zrecv1, ssend0, ssend1, srecv0, srecv1, sall, uall, ufin,
    lsem, ssem, rsem,
):
    d = lax.axis_index("vol")
    g = lax.axis_index("view")
    x, z = d // NZ, d % NZ
    y, c = g // 2, g % 2

    def xp(o):
        return (lax.rem(x + o, NX) * NZ + z, g)

    def zp(o):
        return (x * NZ + lax.rem(z + o, NZ), g)

    def vp(o):
        return (d, lax.rem(g + o, NV))

    def yp(o):
        return (d, lax.rem(y + o, NY) * 2 + c)

    def vq(o, swap):
        return (d, lax.rem(y + o, NY) * 2 + (1 - c if swap else c))

    def xyp(p, o):
        return (lax.rem(x + p, NX) * NZ + z, lax.rem(y + o, NY) * 2 + c)

    core = (d, y * 2 + (1 - c))

    def transfer(src, dst, device, s, r):
        return pltpu.make_async_remote_copy(
            src_ref=src, dst_ref=dst, send_sem=ssem.at[s], recv_sem=rsem.at[r], device_id=device, device_id_type=MESH
        )

    def send(src, dst, device, s, r):
        transfer(src, dst, device, s, r).start()

    def arrived(ref, r):
        transfer(ref, ref, core, 0, r).wait_recv()

    def sent(ref, s):
        transfer(ref, ref, core, s, 0).wait_send()

    barrier = pltpu.get_barrier_semaphore()
    partners = [xp(o) for o in range(1, NX)] + [zp(o) for o in range(1, NZ)] + [vp(o) for o in range(1, NV)]
    partners += [xyp(p, o) for p in range(1, NX) for o in range(1, NY)]
    for device in partners:
        pl.semaphore_signal(barrier, inc=1, device_id=device, device_id_type=MESH)

    own_cols = pl.ds(pl.multiple_of(g * CW, 128), CW)
    fetches = [
        pltpu.make_async_copy(src, dst, lsem.at[n])
        for n, (src, dst) in enumerate((
            (tile_hbm, tile_s), (offset_hbm, offset_s), (angle_hbm, angle_s), (foot_hbm, foot_ref),
            (m_hbm, mraw), (r_hbm, rraw), (c_hbm.at[:, own_cols], cbuf), (vol_hbm, vol_ref),
            (cs_hbm, cs_ref), (c_hbm, cfull),
        ))
    ]
    for copy in fetches[:-1]:
        copy.start()
    tile_in, offset_in, angle_in, foot_in, m_in, r_in, c_in, vol_in, cs_in, cfull_in = fetches

    for copy in (tile_in, offset_in, angle_in, foot_in):
        copy.wait()
    view = lax.broadcasted_iota(jnp.int32, (8, 1), 0)
    start = jnp.zeros((8, 1), jnp.int32)
    angle = jnp.zeros((8, 1), jnp.int32)
    for v in range(8):
        start = jnp.where(view == v, tile_s[0] + offset_s[v], start)
        angle = jnp.where(view == v, angle_s[v], angle)
    foot = jnp.concatenate([jnp.pad(foot_ref[v], ((0, 0), (0, 128 - FR))) for v in range(8)], axis=1)
    f_all = jnp.concatenate(split2(foot), axis=0)
    source = lax.broadcasted_iota(jnp.int32, (128, 1024), 1)
    first = jnp.concatenate([start] * 16, axis=0)
    lane = lax.broadcasted_iota(jnp.int32, (128, 1), 0)
    for zz in range(NZ):
        wanted = (lane // 32) * 32 + zz * 4 + (lane % 32) // 8 - first
        wanted = jnp.where((wanted >= 0) & (wanted < FR), wanted + (lane % 8) * 128, -1)
        one_hot = (source == wanted).astype(F32).astype(BF16)
        placed = lax.dot_general(f_all, one_hot, (((1,), (1,)), ((), ())), preferred_element_type=F32)
        pbuf[zz] = placed[:S] + placed[S:]

    pl.semaphore_wait(barrier, len(partners))

    for o in range(1, NZ):
        send(pbuf.at[lax.rem(z + o, NZ)], gbuf.at[z], zp(o), FZ_S, FZ_R)
    gbuf[z] = pbuf[z]

    shift_back = jnp.where(angle == 0, 0, DC - angle)
    for copy_in, raw, out, got, s, r in ((m_in, mraw, msend, mrecv, M_S, M_R), (r_in, rraw, rsend, rrecv, R_S, R_R)):
        copy_in.wait()
        for i in range(0, 4, 2):
            rolled = [barrel(raw[8 * n : 8 * n + 8, :], shift_back) for n in (i, i + 1)]
            rolled = jnp.concatenate(rolled, axis=0).astype(BF16)
            for k in range(NV):
                out[k, 8 * i : 8 * i + 16, :] = rolled[:, k * CW : (k + 1) * CW]
        for o in (4, 3, 5, 2, 6, 1, 7):
            send(out.at[lax.rem(g + o, NV)], got.at[g], vp(o), s, r)
        got[g] = out[g]

    vol_in.wait()
    v_all = jnp.concatenate(split2(vol_ref[...]), axis=0)
    c_in.wait()
    prod = jnp.dot(v_all, cbuf[...], preferred_element_type=F32)
    own = (prod[:S] + prod[S:]).astype(BF16)
    ybuf0[d] = own[:, :256]
    ybuf1[d] = own[:, 256:]
    for n, o in enumerate((2, 1, 3)):
        send(ybuf1.at[d], ybuf1.at[d], xp(o), Y1X_S, Y1X_R + n)
    for o in range(1, NZ):
        send(ybuf0.at[d], ybuf0.at[d], zp(o), Y0Z_S, Y0Z_R + o - 1)
    for o in (2, 1, 3):
        send(ybuf0.at[d], ybuf0.at[d], xp(o), Y0X_S, Y0X_R)
    for o in range(1, NZ):
        send(ybuf1.at[d], ybuf1.at[d], zp(o), Y1Z_S, Y1Z_R)
    cfull_in.start()

    arrived(gbuf.at[pl.ds(0, NZ - 1)], FZ_R)
    turned = jnp.transpose(gbuf[...].reshape(NZ * S, 128))
    gt[...] = turned.reshape(NX, 32, 128)
    for p, o in [(p, o) for p in (0, 2, 1, 3) for o in (2, 1, 3, 0) if p or o]:
        send(gt.at[lax.rem(x + p, NX)], a4.at[c, y, x], xyp(p, o), F_S + min(p, 1), F_R + p)
    a4[c, y, x] = gt[x]

    for n, o in enumerate((2, 1, 3)):
        tile = lax.rem(x + NX - o, NX) * NZ + z
        arrived(ybuf1.at[tile], Y1X_R + n)
        for p in range(1, NZ):
            send(ybuf1.at[tile], ybuf1.at[tile], zp(p), Y1Z_S, Y1Z_R)
    for o in range(1, NZ):
        tile = x * NZ + lax.rem(z + NZ - o, NZ)
        arrived(ybuf0.at[tile], Y0Z_R + o - 1)
        for p in (2, 1, 3):
            send(ybuf0.at[tile], ybuf0.at[tile], xp(p), Y0X_S, Y0X_R)

    for p in (0, 2, 1, 3):
        column = a4.at[c, :, lax.rem(x + NX - p, NX)]
        arrived(column if p else a4.at[c, pl.ds(0, NY - 1), x], F_R + p)
        send(column, column, core, FC_S, FC_R)
    arrived(a4.at[1 - c], FC_R)

    for k in range(NX):
        part = jnp.concatenate([a4[v % 2, v // 2, k] for v in range(NV)], axis=0)
        hi, lo = split2(part)
        acat[0:256, k * 128 : (k + 1) * 128] = hi
        acat[256:512, k * 128 : (k + 1) * 128] = lo
        atb[k * 128 : (k + 1) * 128, :] = jnp.transpose(part).astype(BF16)

    arrived(ybuf0.at[pl.ds(0, NZ * (NX - 1))], Y0X_R)
    arrived(ybuf1.at[pl.ds(0, NX * (NZ - 1))], Y1Z_R)
    arrived(mrecv.at[pl.ds(0, NV - 1)], M_R)
    arrived(rrecv.at[pl.ds(0, NV - 1)], R_R)
    for j, (first, width) in enumerate(CHUNKS):
        cols = pl.ds(first, width)
        proj = jnp.dot(acat[...], (ybuf0, ybuf1)[j][...].reshape(NX * NZ * S, width), preferred_element_type=F32)
        proj = proj[:256] + proj[256:]
        psend[:, :, cols] = proj.reshape(NV, 32, width)
        measured = mrecv[:, :, cols].astype(F32).reshape(256, width)
        weighted = rrecv[:, :, cols].astype(F32).reshape(256, width) * (measured - proj)
        part = jnp.dot(atb[...], weighted.astype(BF16), preferred_element_type=F32)
        part = part.astype(BF16)
        if j == 0:
            zsend0[...] = part.reshape(NX, 128, width)
            for o in (2, 1, 3):
                send(zsend0.at[lax.rem(x + o, NX)], zrecv0.at[o - 1], xp(o), Z0X_S, Z0X_R)
        else:
            zsend1[...] = part.reshape(NX, NZ, S, width)
            for o in FAR_Z:
                send(zsend1.at[:, lax.rem(z + o, NZ)], zrecv1.at[o - 1], zp(o), Z1Z_S, Z1Z_R)

    for o in (1, 7, 2, 6, 3, 5, 4):
        send(psend.at[lax.rem(g + o, NV)], precv.at[g], vp(o), P_S, P_R)
    precv[g] = psend[g]

    arrived(zrecv0, Z0X_R)
    total = zsend0[x].astype(F32)
    for o in range(NX - 1):
        total += zrecv0[o].astype(F32)
    ssend0[...] = total.astype(BF16).reshape(NZ, S, 256)
    for o in FAR_Z:
        send(ssend0.at[lax.rem(z + o, NZ)], srecv0.at[o - 1], zp(o), Z0Z_S, Z0Z_R)

    arrived(zrecv1, Z1Z_R)
    total = zsend1[:, z].astype(F32)
    for o in range(NZ - 1):
        total += zrecv1[o].astype(F32)
    ssend1[...] = total.astype(BF16)
    for o in (2, 1, 3):
        send(ssend1.at[lax.rem(x + o, NX)], srecv1.at[o - 1], xp(o), Z1X_S, Z1X_R)

    arrived(srecv0, Z0Z_R)
    total = ssend0[z].astype(F32)
    for o in range(NZ - 1):
        total += srecv0[o].astype(F32)
    sall[g, :, :256] = total.astype(BF16)

    arrived(srecv1, Z1X_R)
    total = ssend1[x].astype(F32)
    for o in range(NX - 1):
        total += srecv1[o].astype(F32)
    sall[g, :, 256:] = total.astype(BF16)

    for o in (2, 1, 3):
        for swap in (False, True):
            send(sall.at[g], sall.at[g], vq(o, swap), SV_S, SV_R + o)
    send(sall.at[g], sall.at[g], core, SV_S, SV_R)

    arrived(precv.at[pl.ds(0, NV - 1)], P_R)
    for i in range(4):
        rows = slice(8 * i, 8 * i + 8)
        row = jnp.concatenate([precv[k, rows, :] for k in range(NV)], axis=1)
        wout[rows, :] = rraw[rows, :] * (mraw[rows, :] - barrel(row, angle))
    w_out = pltpu.make_async_copy(wout, wtd_hbm, lsem.at[10])
    w_out.start()

    cfull_in.wait()
    cs_in.wait()
    for o in (0, 1, 3, 2):
        arrived(sall.at[pl.ds(0, 2 if o else 1)], SV_R + o)
        group = lax.rem(y + NY - o, NY)
        both = jnp.concatenate([sall[2 * group], sall[2 * group + 1]], axis=1)
        weights = cfull[:, pl.ds(pl.multiple_of(group * 2 * CW, 128), 2 * CW)]
        uall[group] = lax.dot_general(both, weights, (((1,), (1,)), ((), ())), preferred_element_type=F32)

    total = ((uall[0] + uall[1]) + uall[2]) + uall[3]
    ufin[...] = vol_ref[...] + cs_ref[...] * total
    u_out = pltpu.make_async_copy(ufin, upd_hbm, lsem.at[11])
    u_out.start()
    for ref, s in (
        (gbuf.at[pl.ds(0, NZ - 1)], FZ_S), (mrecv.at[pl.ds(0, NV - 1)], M_S), (rrecv.at[pl.ds(0, NV - 1)], R_S),
        (ybuf1.at[pl.ds(0, NX - 1)], Y1X_S), (ybuf1.at[pl.ds(0, NX * (NZ - 1))], Y1Z_S),
        (ybuf0.at[pl.ds(0, NZ - 1)], Y0Z_S), (ybuf0.at[pl.ds(0, NZ * (NX - 1))], Y0X_S),
        (a4.at[0, 0, pl.ds(0, 3)], F_S), (a4.at[0, :, pl.ds(0, 3)], F_S + 1), (a4.at[0], FC_S),
        (zrecv0, Z0X_S), (zrecv1, Z1Z_S), (srecv0, Z0Z_S), (srecv1, Z1X_S),
        (precv.at[pl.ds(0, NV - 1)], P_S), (sall.at[pl.ds(0, NV - 1)], SV_S),
    ):
        sent(ref, s)
    w_out.wait()
    u_out.wait()


def hand_over(upd_in, wtd_in, upd_out, wtd_out, upd_held, wtd_held, sem):
    pieces = ((wtd_in, wtd_held, wtd_out), (upd_in, upd_held, upd_out))
    arriving = [pltpu.make_async_copy(src, held, sem.at[n]) for n, (src, held, _) in enumerate(pieces)]
    leaving = [pltpu.make_async_copy(held, dst, sem.at[2 + n]) for n, (_, held, dst) in enumerate(pieces)]
    for copy in arriving:
        copy.start()
    for n in range(2):
        arriving[n].wait()
        leaving[n].start()
    for copy in leaving:
        copy.wait()


def body(volume, row_footprint, column_footprint_weights, tile_rows, table_offset, view_angle, measured, row_scale, column_scale):
    foot = jnp.transpose(row_footprint[:, 0], (0, 2, 1))
    hbm = pl.BlockSpec(memory_space=pltpu.HBM)
    updated, weighted = pl.pallas_call(
        kernel,
        out_shape=(jax.ShapeDtypeStruct((S, KV), F32), jax.ShapeDtypeStruct((32, DC), F32)),
        in_specs=[hbm] * 9,
        out_specs=(hbm, hbm),
        scratch_shapes=[
            pltpu.VMEM((S, KV), F32),
            pltpu.VMEM((8, S, FR), F32),
            pltpu.VMEM((S, KV), F32),
            pltpu.SMEM((1,), jnp.int32),
            pltpu.SMEM((8,), jnp.int32),
            pltpu.SMEM((8,), jnp.int32),
            pltpu.VMEM((KV, CW), BF16),
            pltpu.VMEM((KV, DC), BF16),
            pltpu.VMEM((32, DC), F32),
            pltpu.VMEM((32, DC), F32),
            pltpu.VMEM((32, S, 256), BF16),
            pltpu.VMEM((32, S, 128), BF16),
            pltpu.VMEM((NZ, S, 128), F32),
            pltpu.VMEM((NZ, S, 128), F32),
            pltpu.VMEM((NX, 32, 128), F32),
            pltpu.VMEM((2, NY, NX, 32, 128), F32),
            pltpu.VMEM((512, 512), BF16),
            pltpu.VMEM((512, 256), BF16),
            pltpu.VMEM((NV, 32, CW), BF16),
            pltpu.VMEM((NV, 32, CW), BF16),
            pltpu.VMEM((NV, 32, CW), BF16),
            pltpu.VMEM((NV, 32, CW), BF16),
            pltpu.VMEM((NV, 32, CW), F32),
            pltpu.VMEM((NV, 32, CW), F32),
            pltpu.VMEM((32, DC), F32),
            pltpu.VMEM((NX, 128, 256), BF16),
            pltpu.VMEM((NX, NZ, S, 128), BF16),
            pltpu.VMEM((NX - 1, 128, 256), BF16),
            pltpu.VMEM((NZ - 1, NX, S, 128), BF16),
            pltpu.VMEM((NZ, S, 256), BF16),
            pltpu.VMEM((NX, S, 128), BF16),
            pltpu.VMEM((NZ - 1, S, 256), BF16),
            pltpu.VMEM((NX - 1, S, 128), BF16),
            pltpu.VMEM((NV, S, CW), BF16),
            pltpu.VMEM((NY, S, KV), F32),
            pltpu.VMEM((S, KV), F32),
            pltpu.SemaphoreType.DMA((12,)),
            pltpu.SemaphoreType.DMA((N_SENT,)),
            pltpu.SemaphoreType.DMA((N_ARRIVED,)),
        ],
        compiler_params=pltpu.CompilerParams(collective_id=0, has_side_effects=True, vmem_limit_bytes=60 << 20),
        cost_estimate=pl.CostEstimate(flops=500_000_000, bytes_accessed=3_000_000, transcendentals=0),
        name="sirt",
    )(
        volume, foot, column_footprint_weights, tile_rows, table_offset, view_angle,
        measured.reshape(32, DC), row_scale.reshape(32, DC), column_scale,
    )
    return pl.pallas_call(
        hand_over,
        out_shape=(jax.ShapeDtypeStruct((S, KV), F32), jax.ShapeDtypeStruct((4, 8, DC), F32)),
        in_specs=[hbm] * 2,
        out_specs=(hbm, hbm),
        scratch_shapes=[pltpu.VMEM((S, KV), F32), pltpu.VMEM((4, 8, DC), F32), pltpu.SemaphoreType.DMA((4,))],
        compiler_params=pltpu.CompilerParams(vmem_limit_bytes=60 << 20),
        name="hand_over",
    )(updated, weighted.reshape(4, 8, DC))


def solution(mesh):
    placed = (
        P(None, "vol"),
        P("view", "vol", None, None),
        P("vol", None),
        P("vol"),
        P("view"),
        P("view"),
        P("vol", "view", None),
        P("vol", "view", None),
        P(None, "vol"),
    )
    return jax.shard_map(
        body,
        mesh=mesh,
        in_specs=placed,
        out_specs=(P(None, "vol"), P("vol", "view", None)),
        check_vma=False,
    )
```

```python
import functools

import jax
import jax.numpy as jnp
from jax import lax
from jax.experimental import pallas as pl
from jax.experimental.pallas import tpu as pltpu
from jax.sharding import PartitionSpec as P

MESH = pl.DeviceIdType.MESH
F32, BF16 = jnp.float32, jnp.bfloat16
S, FR, DR, DC, KV = 16, 80, 128, 3072, 1024
NX, NY, NZ, NV = 4, 4, 8, 8
CW = DC // 8
CHUNKS = ((0, 256), (256, 128))
FAR_Z = (4, 3, 5, 2, 6, 1, 7)
(FZ_S, M_S, R_S, Y1X_S, Y1Z_S, Y0Z_S, Y0X_S, F_S, _, FC_S, Z0X_S, Z1Z_S, Z0Z_S, Z1X_S, P_S, SV_S) = range(16)
(FZ_R, M_R, R_R, Y1Z_R, Y0X_R, FC_R, Z0X_R, Z1Z_R, Z0Z_R, Z1X_R, P_R) = range(11)
Y1X_R, Y0Z_R, F_R, SV_R = 11, 14, 21, 25
N_SENT, N_ARRIVED = 16, 29


def split2(a):
    hi = a.astype(BF16)
    return hi, (a - hi.astype(F32)).astype(BF16)


def barrel(a, shift):
    for bit in range(12):
        moved = pltpu.roll(a, 1 << bit, 1)
        on = jnp.broadcast_to((shift >> bit) & 1, a.shape)
        a = jnp.where(on == 1, moved, a)
    return a


def kernel(
    vol_hbm, foot_hbm, c_hbm, tile_hbm, offset_hbm, angle_hbm, m_hbm, r_hbm, cs_hbm,
    upd_hbm, wtd_hbm,
    vol_ref, foot_ref, cs_ref, tile_s, offset_s, angle_s, cbuf, cfull, mraw, rraw, ybuf0, ybuf1, pbuf, gbuf, gt, a4, acat, atb,
    msend, rsend, mrecv, rrecv, psend, precv, wout,
    zsend0, zsend1, zrecv0, zrecv1, ssend0, ssend1, srecv0, srecv1, sall, uall, ufin,
    lsem, ssem, rsem,
):
    d = lax.axis_index("vol")
    g = lax.axis_index("view")
    x, z = d // NZ, d % NZ
    y, c = g // 2, g % 2

    def xp(o):
        return (lax.rem(x + o, NX) * NZ + z, g)

    def zp(o):
        return (x * NZ + lax.rem(z + o, NZ), g)

    def vp(o):
        return (d, lax.rem(g + o, NV))

    def yp(o):
        return (d, lax.rem(y + o, NY) * 2 + c)

    def vq(o, swap):
        return (d, lax.rem(y + o, NY) * 2 + (1 - c if swap else c))

    def xyp(p, o):
        return (lax.rem(x + p, NX) * NZ + z, lax.rem(y + o, NY) * 2 + c)

    core = (d, y * 2 + (1 - c))

    def transfer(src, dst, device, s, r):
        return pltpu.make_async_remote_copy(
            src_ref=src, dst_ref=dst, send_sem=ssem.at[s], recv_sem=rsem.at[r], device_id=device, device_id_type=MESH
        )

    def send(src, dst, device, s, r):
        transfer(src, dst, device, s, r).start()

    def arrived(ref, r):
        transfer(ref, ref, core, 0, r).wait_recv()

    def sent(ref, s):
        transfer(ref, ref, core, s, 0).wait_send()

    barrier = pltpu.get_barrier_semaphore()
    partners = [xp(o) for o in range(1, NX)] + [zp(o) for o in range(1, NZ)] + [vp(o) for o in range(1, NV)]
    partners += [xyp(p, o) for p in range(1, NX) for o in range(1, NY)]
    for device in partners:
        pl.semaphore_signal(barrier, inc=1, device_id=device, device_id_type=MESH)

    own_cols = pl.ds(pl.multiple_of(g * CW, 128), CW)
    fetches = [
        pltpu.make_async_copy(src, dst, lsem.at[n])
        for n, (src, dst) in enumerate((
            (tile_hbm, tile_s), (offset_hbm, offset_s), (angle_hbm, angle_s), (foot_hbm, foot_ref),
            (m_hbm, mraw), (r_hbm, rraw), (c_hbm.at[:, own_cols], cbuf), (vol_hbm, vol_ref),
            (cs_hbm, cs_ref), (c_hbm, cfull),
        ))
    ]
    for copy in fetches[:-1]:
        copy.start()
    tile_in, offset_in, angle_in, foot_in, m_in, r_in, c_in, vol_in, cs_in, cfull_in = fetches

    for copy in (tile_in, offset_in, angle_in, foot_in):
        copy.wait()
    view = lax.broadcasted_iota(jnp.int32, (8, 1), 0)
    start = jnp.zeros((8, 1), jnp.int32)
    angle = jnp.zeros((8, 1), jnp.int32)
    for v in range(8):
        start = jnp.where(view == v, tile_s[0] + offset_s[v], start)
        angle = jnp.where(view == v, angle_s[v], angle)
    foot = jnp.concatenate([jnp.pad(foot_ref[v], ((0, 0), (0, 128 - FR))) for v in range(8)], axis=1)
    f_all = jnp.concatenate(split2(foot), axis=0)
    source = lax.broadcasted_iota(jnp.int32, (128, 1024), 1)
    first = jnp.concatenate([start] * 16, axis=0)
    lane = lax.broadcasted_iota(jnp.int32, (128, 1), 0)
    for zz in range(NZ):
        wanted = (lane // 32) * 32 + zz * 4 + (lane % 32) // 8 - first
        wanted = jnp.where((wanted >= 0) & (wanted < FR), wanted + (lane % 8) * 128, -1)
        one_hot = (source == wanted).astype(F32).astype(BF16)
        placed = lax.dot_general(f_all, one_hot, (((1,), (1,)), ((), ())), preferred_element_type=F32)
        placed = placed[:S] + placed[S:]
        pbuf[zz] = (placed * placed).astype(BF16)

    pl.semaphore_wait(barrier, len(partners))

    for o in range(1, NZ):
        send(pbuf.at[lax.rem(z + o, NZ)], gbuf.at[z], zp(o), FZ_S, FZ_R)
    gbuf[z] = pbuf[z]

    vol_in.wait()
    v_all = jnp.concatenate(split2(vol_ref[...]), axis=0)
    c_in.wait()
    prod = jnp.dot(v_all, cbuf[...], preferred_element_type=F32)
    own = (prod[:S] + prod[S:]).astype(BF16)
    ybuf0[d] = own[:, :256]
    ybuf1[d] = own[:, 256:]
    for n, o in enumerate((2, 1, 3)):
        send(ybuf1.at[d], ybuf1.at[d], xp(o), Y1X_S, Y1X_R + n)
    for o in range(1, NZ):
        send(ybuf0.at[d], ybuf0.at[d], zp(o), Y0Z_S, Y0Z_R + o - 1)
    for o in (2, 1, 3):
        send(ybuf0.at[d], ybuf0.at[d], xp(o), Y0X_S, Y0X_R)
    for o in range(1, NZ):
        send(ybuf1.at[d], ybuf1.at[d], zp(o), Y1Z_S, Y1Z_R)

    shift_back = jnp.where(angle == 0, 0, DC - angle)
    for copy_in, raw, out, got, s, r in ((m_in, mraw, msend, mrecv, M_S, M_R), (r_in, rraw, rsend, rrecv, R_S, R_R)):
        copy_in.wait()
        for i in range(0, 4, 2):
            rolled = [barrel(raw[8 * n : 8 * n + 8, :], shift_back) for n in (i, i + 1)]
            rolled = jnp.concatenate(rolled, axis=0).astype(BF16)
            for k in range(NV):
                out[k, 8 * i : 8 * i + 16, :] = rolled[:, k * CW : (k + 1) * CW]
        for o in (4, 3, 5, 2, 6, 1, 7):
            send(out.at[lax.rem(g + o, NV)], got.at[g], vp(o), s, r)
        got[g] = out[g]
    cfull_in.start()

    arrived(gbuf.at[pl.ds(0, NZ - 1)], FZ_R)
    turned = jnp.transpose(gbuf[...].astype(F32).reshape(NZ * S, 128))
    gt[...] = turned.astype(BF16).reshape(NX, 32, 128)
    for p, o in [(p, o) for p in (0, 2, 1, 3) for o in (2, 1, 3, 0) if p or o]:
        send(gt.at[lax.rem(x + p, NX)], a4.at[c, y, x], xyp(p, o), F_S + min(p, 1), F_R + p)
    a4[c, y, x] = gt[x]

    for n, o in enumerate((2, 1, 3)):
        tile = lax.rem(x + NX - o, NX) * NZ + z
        arrived(ybuf1.at[tile], Y1X_R + n)
        for p in range(1, NZ):
            send(ybuf1.at[tile], ybuf1.at[tile], zp(p), Y1Z_S, Y1Z_R)
    for o in range(1, NZ):
        tile = x * NZ + lax.rem(z + NZ - o, NZ)
        arrived(ybuf0.at[tile], Y0Z_R + o - 1)
        for p in (2, 1, 3):
            send(ybuf0.at[tile], ybuf0.at[tile], xp(p), Y0X_S, Y0X_R)

    for p in (0, 2, 1, 3):
        column = a4.at[c, :, lax.rem(x + NX - p, NX)]
        arrived(column if p else a4.at[c, pl.ds(0, NY - 1), x], F_R + p)
        send(column, column, core, FC_S, FC_R)
    arrived(a4.at[1 - c], FC_R)

    for k in range(NX):
        part = jnp.sqrt(jnp.concatenate([a4[v % 2, v // 2, k] for v in range(NV)], axis=0).astype(F32))
        hi, lo = split2(part)
        acat[0:256, k * 128 : (k + 1) * 128] = hi
        acat[256:512, k * 128 : (k + 1) * 128] = lo
        atb[k * 128 : (k + 1) * 128, :] = jnp.transpose(part).astype(BF16)

    arrived(ybuf0.at[pl.ds(0, NZ * (NX - 1))], Y0X_R)
    arrived(ybuf1.at[pl.ds(0, NX * (NZ - 1))], Y1Z_R)
    arrived(mrecv.at[pl.ds(0, NV - 1)], M_R)
    arrived(rrecv.at[pl.ds(0, NV - 1)], R_R)
    for j, (first, width) in enumerate(CHUNKS):
        cols = pl.ds(first, width)
        proj = jnp.dot(acat[...], (ybuf0, ybuf1)[j][...].reshape(NX * NZ * S, width), preferred_element_type=F32)
        proj = proj[:256] + proj[256:]
        psend[:, :, cols] = proj.reshape(NV, 32, width)
        measured = mrecv[:, :, cols].astype(F32).reshape(256, width)
        weighted = rrecv[:, :, cols].astype(F32).reshape(256, width) * (measured - proj)
        part = jnp.dot(atb[...], weighted.astype(BF16), preferred_element_type=F32)
        part = part.astype(BF16)
        if j == 0:
            zsend0[...] = part.reshape(NX, 128, width)
            for o in (2, 1, 3):
                send(zsend0.at[lax.rem(x + o, NX)], zrecv0.at[o - 1], xp(o), Z0X_S, Z0X_R)
        else:
            zsend1[...] = part.reshape(NX, NZ, S, width)
            for o in FAR_Z:
                send(zsend1.at[:, lax.rem(z + o, NZ)], zrecv1.at[o - 1], zp(o), Z1Z_S, Z1Z_R)

    for o in (1, 7, 2, 6, 3, 5, 4):
        send(psend.at[lax.rem(g + o, NV)], precv.at[g], vp(o), P_S, P_R)
    precv[g] = psend[g]

    arrived(zrecv0, Z0X_R)
    total = zsend0[x].astype(F32)
    for o in range(NX - 1):
        total += zrecv0[o].astype(F32)
    ssend0[...] = total.astype(BF16).reshape(NZ, S, 256)
    for o in FAR_Z:
        send(ssend0.at[lax.rem(z + o, NZ)], srecv0.at[o - 1], zp(o), Z0Z_S, Z0Z_R)

    arrived(zrecv1, Z1Z_R)
    total = zsend1[:, z].astype(F32)
    for o in range(NZ - 1):
        total += zrecv1[o].astype(F32)
    ssend1[...] = total.astype(BF16)
    for o in (2, 1, 3):
        send(ssend1.at[lax.rem(x + o, NX)], srecv1.at[o - 1], xp(o), Z1X_S, Z1X_R)

    arrived(srecv0, Z0Z_R)
    total = ssend0[z].astype(F32)
    for o in range(NZ - 1):
        total += srecv0[o].astype(F32)
    sall[g, :, :256] = total.astype(BF16)

    arrived(srecv1, Z1X_R)
    total = ssend1[x].astype(F32)
    for o in range(NX - 1):
        total += srecv1[o].astype(F32)
    sall[g, :, 256:] = total.astype(BF16)

    for o in (2, 1, 3):
        for swap in (False, True):
            send(sall.at[g], sall.at[g], vq(o, swap), SV_S, SV_R + o)
    send(sall.at[g], sall.at[g], core, SV_S, SV_R)

    arrived(precv.at[pl.ds(0, NV - 1)], P_R)
    for i in range(4):
        rows = slice(8 * i, 8 * i + 8)
        row = jnp.concatenate([precv[k, rows, :] for k in range(NV)], axis=1)
        wout[rows, :] = rraw[rows, :] * (mraw[rows, :] - barrel(row, angle))
    w_out = pltpu.make_async_copy(wout, wtd_hbm, lsem.at[10])
    w_out.start()

    cfull_in.wait()
    cs_in.wait()
    for o in (0, 1, 3, 2):
        arrived(sall.at[pl.ds(0, 2 if o else 1)], SV_R + o)
        group = lax.rem(y + NY - o, NY)
        both = jnp.concatenate([sall[2 * group], sall[2 * group + 1]], axis=1)
        weights = cfull[:, pl.ds(pl.multiple_of(group * 2 * CW, 128), 2 * CW)]
        uall[group] = lax.dot_general(both, weights, (((1,), (1,)), ((), ())), preferred_element_type=F32)

    total = ((uall[0] + uall[1]) + uall[2]) + uall[3]
    ufin[...] = vol_ref[...] + cs_ref[...] * total
    u_out = pltpu.make_async_copy(ufin, upd_hbm, lsem.at[11])
    u_out.start()
    for ref, s in (
        (gbuf.at[pl.ds(0, NZ - 1)], FZ_S), (mrecv.at[pl.ds(0, NV - 1)], M_S), (rrecv.at[pl.ds(0, NV - 1)], R_S),
        (ybuf1.at[pl.ds(0, NX - 1)], Y1X_S), (ybuf1.at[pl.ds(0, NX * (NZ - 1))], Y1Z_S),
        (ybuf0.at[pl.ds(0, NZ - 1)], Y0Z_S), (ybuf0.at[pl.ds(0, NZ * (NX - 1))], Y0X_S),
        (a4.at[0, 0, pl.ds(0, 3)], F_S), (a4.at[0, :, pl.ds(0, 3)], F_S + 1), (a4.at[0], FC_S),
        (zrecv0, Z0X_S), (zrecv1, Z1Z_S), (srecv0, Z0Z_S), (srecv1, Z1X_S),
        (precv.at[pl.ds(0, NV - 1)], P_S), (sall.at[pl.ds(0, NV - 1)], SV_S),
    ):
        sent(ref, s)
    w_out.wait()
    u_out.wait()


def hand_over(upd_in, wtd_in, upd_out, wtd_out, upd_held, wtd_held, sem):
    pieces = ((wtd_in, wtd_held, wtd_out), (upd_in, upd_held, upd_out))
    arriving = [pltpu.make_async_copy(src, held, sem.at[n]) for n, (src, held, _) in enumerate(pieces)]
    leaving = [pltpu.make_async_copy(held, dst, sem.at[2 + n]) for n, (_, held, dst) in enumerate(pieces)]
    for copy in arriving:
        copy.start()
    for n in range(2):
        arriving[n].wait()
        leaving[n].start()
    for copy in leaving:
        copy.wait()


def body(volume, row_footprint, column_footprint_weights, tile_rows, table_offset, view_angle, measured, row_scale, column_scale):
    foot = jnp.transpose(row_footprint[:, 0], (0, 2, 1))
    hbm = pl.BlockSpec(memory_space=pltpu.HBM)
    updated, weighted = pl.pallas_call(
        kernel,
        out_shape=(jax.ShapeDtypeStruct((S, KV), F32), jax.ShapeDtypeStruct((32, DC), F32)),
        in_specs=[hbm] * 9,
        out_specs=(hbm, hbm),
        scratch_shapes=[
            pltpu.VMEM((S, KV), F32),
            pltpu.VMEM((8, S, FR), F32),
            pltpu.VMEM((S, KV), F32),
            pltpu.SMEM((1,), jnp.int32),
            pltpu.SMEM((8,), jnp.int32),
            pltpu.SMEM((8,), jnp.int32),
            pltpu.VMEM((KV, CW), BF16),
            pltpu.VMEM((KV, DC), BF16),
            pltpu.VMEM((32, DC), F32),
            pltpu.VMEM((32, DC), F32),
            pltpu.VMEM((32, S, 256), BF16),
            pltpu.VMEM((32, S, 128), BF16),
            pltpu.VMEM((NZ, S, 128), BF16),
            pltpu.VMEM((NZ, S, 128), BF16),
            pltpu.VMEM((NX, 32, 128), BF16),
            pltpu.VMEM((2, NY, NX, 32, 128), BF16),
            pltpu.VMEM((512, 512), BF16),
            pltpu.VMEM((512, 256), BF16),
            pltpu.VMEM((NV, 32, CW), BF16),
            pltpu.VMEM((NV, 32, CW), BF16),
            pltpu.VMEM((NV, 32, CW), BF16),
            pltpu.VMEM((NV, 32, CW), BF16),
            pltpu.VMEM((NV, 32, CW), F32),
            pltpu.VMEM((NV, 32, CW), F32),
            pltpu.VMEM((32, DC), F32),
            pltpu.VMEM((NX, 128, 256), BF16),
            pltpu.VMEM((NX, NZ, S, 128), BF16),
            pltpu.VMEM((NX - 1, 128, 256), BF16),
            pltpu.VMEM((NZ - 1, NX, S, 128), BF16),
            pltpu.VMEM((NZ, S, 256), BF16),
            pltpu.VMEM((NX, S, 128), BF16),
            pltpu.VMEM((NZ - 1, S, 256), BF16),
            pltpu.VMEM((NX - 1, S, 128), BF16),
            pltpu.VMEM((NV, S, CW), BF16),
            pltpu.VMEM((NY, S, KV), F32),
            pltpu.VMEM((S, KV), F32),
            pltpu.SemaphoreType.DMA((12,)),
            pltpu.SemaphoreType.DMA((N_SENT,)),
            pltpu.SemaphoreType.DMA((N_ARRIVED,)),
        ],
        compiler_params=pltpu.CompilerParams(collective_id=0, has_side_effects=True, vmem_limit_bytes=60 << 20),
        cost_estimate=pl.CostEstimate(flops=500_000_000, bytes_accessed=3_000_000, transcendentals=0),
        name="sirt",
    )(
        volume, foot, column_footprint_weights, tile_rows, table_offset, view_angle,
        measured.reshape(32, DC), row_scale.reshape(32, DC), column_scale,
    )
    return pl.pallas_call(
        hand_over,
        out_shape=(jax.ShapeDtypeStruct((S, KV), F32), jax.ShapeDtypeStruct((4, 8, DC), F32)),
        in_specs=[hbm] * 2,
        out_specs=(hbm, hbm),
        scratch_shapes=[pltpu.VMEM((S, KV), F32), pltpu.VMEM((4, 8, DC), F32), pltpu.SemaphoreType.DMA((4,))],
        compiler_params=pltpu.CompilerParams(vmem_limit_bytes=60 << 20),
        name="hand_over",
    )(updated, weighted.reshape(4, 8, DC))


def solution(mesh):
    placed = (
        P(None, "vol"),
        P("view", "vol", None, None),
        P("vol", None),
        P("vol"),
        P("view"),
        P("view"),
        P("vol", "view", None),
        P("vol", "view", None),
        P(None, "vol"),
    )
    return jax.shard_map(
        body,
        mesh=mesh,
        in_specs=placed,
        out_specs=(P(None, "vol"), P("vol", "view", None)),
        check_vma=False,
    )
```

```python
import functools

import jax
import jax.numpy as jnp
from jax import lax
from jax.experimental import pallas as pl
from jax.experimental.pallas import tpu as pltpu
from jax.sharding import PartitionSpec as P

MESH = pl.DeviceIdType.MESH
F32, BF16 = jnp.float32, jnp.bfloat16
S, FR, DR, DC, KV = 16, 80, 128, 3072, 1024
NX, NY, NZ, NV = 4, 4, 8, 8
CW = DC // 8
CHUNKS = ((0, 256), (256, 128))
FAR_Z = (4, 3, 5, 2, 6, 1, 7)
(FZ_S, M_S, R_S, Y1X_S, Y1Z_S, Y0Z_S, Y0X_S, F_S, _, FC_S, Z0X_S, Z1Z_S, Z0Z_S, Z1X_S, P_S, SV_S) = range(16)
(FZ_R, M_R, R_R, Y1Z_R, Y0X_R, FC_R, Z0X_R, Z1Z_R, Z0Z_R, Z1X_R, P_R) = range(11)
Y1X_R, Y0Z_R, F_R, SV_R = 11, 14, 21, 25
N_SENT, N_ARRIVED = 16, 29


def split2(a):
    hi = a.astype(BF16)
    return hi, (a - hi.astype(F32)).astype(BF16)


def barrel(a, shift):
    for bit in range(12):
        moved = pltpu.roll(a, 1 << bit, 1)
        on = jnp.broadcast_to((shift >> bit) & 1, a.shape)
        a = jnp.where(on == 1, moved, a)
    return a


def kernel(
    vol_hbm, foot_hbm, c_hbm, tile_hbm, offset_hbm, angle_hbm, m_hbm, r_hbm, cs_hbm,
    upd_ref, wtd_ref,
    vol_ref, foot_ref, cs_ref, tile_s, offset_s, angle_s, cbuf, cfull, mraw, rraw, ybuf0, ybuf1, pbuf, gbuf, gt, a4, acat, atb,
    msend, rsend, mrecv, rrecv, psend, precv,
    zsend0, zsend1, zrecv0, zrecv1, ssend0, ssend1, srecv0, srecv1, sall, uall,
    lsem, ssem, rsem,
):
    d = lax.axis_index("vol")
    g = lax.axis_index("view")
    x, z = d // NZ, d % NZ
    y, c = g // 2, g % 2

    def xp(o):
        return (lax.rem(x + o, NX) * NZ + z, g)

    def zp(o):
        return (x * NZ + lax.rem(z + o, NZ), g)

    def vp(o):
        return (d, lax.rem(g + o, NV))

    def yp(o):
        return (d, lax.rem(y + o, NY) * 2 + c)

    def vq(o, swap):
        return (d, lax.rem(y + o, NY) * 2 + (1 - c if swap else c))

    def xyp(p, o):
        return (lax.rem(x + p, NX) * NZ + z, lax.rem(y + o, NY) * 2 + c)

    core = (d, y * 2 + (1 - c))

    def transfer(src, dst, device, s, r):
        return pltpu.make_async_remote_copy(
            src_ref=src, dst_ref=dst, send_sem=ssem.at[s], recv_sem=rsem.at[r], device_id=device, device_id_type=MESH
        )

    def send(src, dst, device, s, r):
        transfer(src, dst, device, s, r).start()

    def arrived(ref, r):
        transfer(ref, ref, core, 0, r).wait_recv()

    def sent(ref, s):
        transfer(ref, ref, core, s, 0).wait_send()

    barrier = pltpu.get_barrier_semaphore()
    partners = [xp(o) for o in range(1, NX)] + [zp(o) for o in range(1, NZ)] + [vp(o) for o in range(1, NV)]
    partners += [xyp(p, o) for p in range(1, NX) for o in range(1, NY)]
    for device in partners:
        pl.semaphore_signal(barrier, inc=1, device_id=device, device_id_type=MESH)

    own_cols = pl.ds(pl.multiple_of(g * CW, 128), CW)
    fetches = [
        pltpu.make_async_copy(src, dst, lsem.at[n])
        for n, (src, dst) in enumerate((
            (tile_hbm, tile_s), (offset_hbm, offset_s), (angle_hbm, angle_s), (foot_hbm, foot_ref),
            (m_hbm, mraw), (r_hbm, rraw), (c_hbm.at[:, own_cols], cbuf), (vol_hbm, vol_ref),
            (cs_hbm, cs_ref), (c_hbm, cfull),
        ))
    ]
    for copy in fetches[:-1]:
        copy.start()
    tile_in, offset_in, angle_in, foot_in, m_in, r_in, c_in, vol_in, cs_in, cfull_in = fetches

    for copy in (tile_in, offset_in, angle_in, foot_in):
        copy.wait()
    view = lax.broadcasted_iota(jnp.int32, (8, 1), 0)
    start = jnp.zeros((8, 1), jnp.int32)
    angle = jnp.zeros((8, 1), jnp.int32)
    for v in range(8):
        start = jnp.where(view == v, tile_s[0] + offset_s[v], start)
        angle = jnp.where(view == v, angle_s[v], angle)
    foot = jnp.concatenate([jnp.pad(foot_ref[v], ((0, 0), (0, 128 - FR))) for v in range(8)], axis=1)
    f_all = jnp.concatenate(split2(foot), axis=0)
    source = lax.broadcasted_iota(jnp.int32, (128, 1024), 1)
    first = jnp.concatenate([start] * 16, axis=0)
    lane = lax.broadcasted_iota(jnp.int32, (128, 1), 0)
    for zz in range(NZ):
        wanted = (lane // 32) * 32 + zz * 4 + (lane % 32) // 8 - first
        wanted = jnp.where((wanted >= 0) & (wanted < FR), wanted + (lane % 8) * 128, -1)
        one_hot = (source == wanted).astype(F32).astype(BF16)
        placed = lax.dot_general(f_all, one_hot, (((1,), (1,)), ((), ())), preferred_element_type=F32)
        placed = placed[:S] + placed[S:]
        pbuf[zz] = (placed * placed).astype(BF16)

    pl.semaphore_wait(barrier, len(partners))

    for o in range(1, NZ):
        send(pbuf.at[lax.rem(z + o, NZ)], gbuf.at[z], zp(o), FZ_S, FZ_R)
    gbuf[z] = pbuf[z]

    vol_in.wait()
    v_all = jnp.concatenate(split2(vol_ref[...]), axis=0)
    c_in.wait()
    prod = jnp.dot(v_all, cbuf[...], preferred_element_type=F32)
    own = (prod[:S] + prod[S:]).astype(BF16)
    ybuf0[d] = own[:, :256]
    ybuf1[d] = own[:, 256:]
    for n, o in enumerate((2, 1, 3)):
        send(ybuf1.at[d], ybuf1.at[d], xp(o), Y1X_S, Y1X_R + n)
    for o in range(1, NZ):
        send(ybuf0.at[d], ybuf0.at[d], zp(o), Y0Z_S, Y0Z_R + o - 1)
    for o in (2, 1, 3):
        send(ybuf0.at[d], ybuf0.at[d], xp(o), Y0X_S, Y0X_R)
    for o in range(1, NZ):
        send(ybuf1.at[d], ybuf1.at[d], zp(o), Y1Z_S, Y1Z_R)

    shift_back = jnp.where(angle == 0, 0, DC - angle)
    for copy_in, raw, out, got, s, r in ((m_in, mraw, msend, mrecv, M_S, M_R), (r_in, rraw, rsend, rrecv, R_S, R_R)):
        copy_in.wait()
        for i in range(0, 4, 2):
            rolled = [barrel(raw[8 * n : 8 * n + 8, :], shift_back) for n in (i, i + 1)]
            rolled = jnp.concatenate(rolled, axis=0).astype(BF16)
            for k in range(NV):
                out[k, 8 * i : 8 * i + 16, :] = rolled[:, k * CW : (k + 1) * CW]
        for o in (4, 3, 5, 2, 6, 1, 7):
            send(out.at[lax.rem(g + o, NV)], got.at[g], vp(o), s, r)
        got[g] = out[g]
    cfull_in.start()

    arrived(gbuf.at[pl.ds(0, NZ - 1)], FZ_R)
    turned = jnp.transpose(gbuf[...].astype(F32).reshape(NZ * S, 128))
    gt[...] = turned.astype(BF16).reshape(NX, 32, 128)
    for p, o in [(p, o) for p in (0, 2, 1, 3) for o in (2, 1, 3, 0) if p or o]:
        send(gt.at[lax.rem(x + p, NX)], a4.at[c, y, x], xyp(p, o), F_S + min(p, 1), F_R + p)
    a4[c, y, x] = gt[x]

    for n, o in enumerate((2, 1, 3)):
        tile = lax.rem(x + NX - o, NX) * NZ + z
        arrived(ybuf1.at[tile], Y1X_R + n)
        for p in range(1, NZ):
            send(ybuf1.at[tile], ybuf1.at[tile], zp(p), Y1Z_S, Y1Z_R)
    for o in range(1, NZ):
        tile = x * NZ + lax.rem(z + NZ - o, NZ)
        arrived(ybuf0.at[tile], Y0Z_R + o - 1)
        for p in (2, 1, 3):
            send(ybuf0.at[tile], ybuf0.at[tile], xp(p), Y0X_S, Y0X_R)

    for p in (0, 2, 1, 3):
        column = a4.at[c, :, lax.rem(x + NX - p, NX)]
        arrived(column if p else a4.at[c, pl.ds(0, NY - 1), x], F_R + p)
        send(column, column, core, FC_S, FC_R)
    arrived(a4.at[1 - c], FC_R)

    for k in range(NX):
        part = jnp.sqrt(jnp.concatenate([a4[v % 2, v // 2, k] for v in range(NV)], axis=0).astype(F32))
        hi, lo = split2(part)
        acat[0:256, k * 128 : (k + 1) * 128] = hi
        acat[256:512, k * 128 : (k + 1) * 128] = lo
        atb[k * 128 : (k + 1) * 128, :] = jnp.transpose(part).astype(BF16)

    arrived(ybuf0.at[pl.ds(0, NZ * (NX - 1))], Y0X_R)
    arrived(ybuf1.at[pl.ds(0, NX * (NZ - 1))], Y1Z_R)
    arrived(mrecv.at[pl.ds(0, NV - 1)], M_R)
    arrived(rrecv.at[pl.ds(0, NV - 1)], R_R)
    for j, (first, width) in enumerate(CHUNKS):
        cols = pl.ds(first, width)
        proj = jnp.dot(acat[...], (ybuf0, ybuf1)[j][...].reshape(NX * NZ * S, width), preferred_element_type=F32)
        proj = proj[:256] + proj[256:]
        psend[:, :, cols] = proj.reshape(NV, 32, width)
        measured = mrecv[:, :, cols].astype(F32).reshape(256, width)
        weighted = rrecv[:, :, cols].astype(F32).reshape(256, width) * (measured - proj)
        part = jnp.dot(atb[...], weighted.astype(BF16), preferred_element_type=F32)
        part = part.astype(BF16)
        if j == 0:
            zsend0[...] = part.reshape(NX, 128, width)
            for o in (2, 1, 3):
                send(zsend0.at[lax.rem(x + o, NX)], zrecv0.at[o - 1], xp(o), Z0X_S, Z0X_R)
        else:
            zsend1[...] = part.reshape(NX, NZ, S, width)
            for o in FAR_Z:
                send(zsend1.at[:, lax.rem(z + o, NZ)], zrecv1.at[o - 1], zp(o), Z1Z_S, Z1Z_R)

    for o in (1, 7, 2, 6, 3, 5, 4):
        send(psend.at[lax.rem(g + o, NV)], precv.at[g], vp(o), P_S, P_R)
    precv[g] = psend[g]

    arrived(zrecv0, Z0X_R)
    total = zsend0[x].astype(F32)
    for o in range(NX - 1):
        total += zrecv0[o].astype(F32)
    ssend0[...] = total.astype(BF16).reshape(NZ, S, 256)
    for o in FAR_Z:
        send(ssend0.at[lax.rem(z + o, NZ)], srecv0.at[o - 1], zp(o), Z0Z_S, Z0Z_R)

    arrived(zrecv1, Z1Z_R)
    total = zsend1[:, z].astype(F32)
    for o in range(NZ - 1):
        total += zrecv1[o].astype(F32)
    ssend1[...] = total.astype(BF16)
    for o in (2, 1, 3):
        send(ssend1.at[lax.rem(x + o, NX)], srecv1.at[o - 1], xp(o), Z1X_S, Z1X_R)

    arrived(srecv0, Z0Z_R)
    total = ssend0[z].astype(F32)
    for o in range(NZ - 1):
        total += srecv0[o].astype(F32)
    sall[g, :, :256] = total.astype(BF16)

    arrived(srecv1, Z1X_R)
    total = ssend1[x].astype(F32)
    for o in range(NX - 1):
        total += srecv1[o].astype(F32)
    sall[g, :, 256:] = total.astype(BF16)

    for o in (2, 1, 3):
        for swap in (False, True):
            send(sall.at[g], sall.at[g], vq(o, swap), SV_S, SV_R + o)
    send(sall.at[g], sall.at[g], core, SV_S, SV_R)

    arrived(precv.at[pl.ds(0, NV - 1)], P_R)
    for i in range(4):
        rows = slice(8 * i, 8 * i + 8)
        row = jnp.concatenate([precv[k, rows, :] for k in range(NV)], axis=1)
        wtd_ref[rows, :] = rraw[rows, :] * (mraw[rows, :] - barrel(row, angle))

    cfull_in.wait()
    cs_in.wait()
    for o in (0, 1, 3, 2):
        arrived(sall.at[pl.ds(0, 2 if o else 1)], SV_R + o)
        group = lax.rem(y + NY - o, NY)
        both = jnp.concatenate([sall[2 * group], sall[2 * group + 1]], axis=1)
        weights = cfull[:, pl.ds(pl.multiple_of(group * 2 * CW, 128), 2 * CW)]
        uall[group] = lax.dot_general(both, weights, (((1,), (1,)), ((), ())), preferred_element_type=F32)

    total = ((uall[0] + uall[1]) + uall[2]) + uall[3]
    upd_ref[...] = vol_ref[...] + cs_ref[...] * total
    for ref, s in (
        (gbuf.at[pl.ds(0, NZ - 1)], FZ_S), (mrecv.at[pl.ds(0, NV - 1)], M_S), (rrecv.at[pl.ds(0, NV - 1)], R_S),
        (ybuf1.at[pl.ds(0, NX - 1)], Y1X_S), (ybuf1.at[pl.ds(0, NX * (NZ - 1))], Y1Z_S),
        (ybuf0.at[pl.ds(0, NZ - 1)], Y0Z_S), (ybuf0.at[pl.ds(0, NZ * (NX - 1))], Y0X_S),
        (a4.at[0, 0, pl.ds(0, 3)], F_S), (a4.at[0, :, pl.ds(0, 3)], F_S + 1), (a4.at[0], FC_S),
        (zrecv0, Z0X_S), (zrecv1, Z1Z_S), (srecv0, Z0Z_S), (srecv1, Z1X_S),
        (precv.at[pl.ds(0, NV - 1)], P_S), (sall.at[pl.ds(0, NV - 1)], SV_S),
    ):
        sent(ref, s)


def hand_over(upd_in, wtd_in, upd_out, wtd_out, sem):
    copies = (pltpu.make_async_copy(wtd_in, wtd_out, sem.at[0]), pltpu.make_async_copy(upd_in, upd_out, sem.at[1]))
    for copy in copies:
        copy.start()
    for copy in copies:
        copy.wait()


def body(volume, row_footprint, column_footprint_weights, tile_rows, table_offset, view_angle, measured, row_scale, column_scale):
    foot = jnp.transpose(row_footprint[:, 0], (0, 2, 1))
    hbm = pl.BlockSpec(memory_space=pltpu.HBM)
    vmem = pl.BlockSpec(memory_space=pltpu.VMEM)
    updated, weighted = pl.pallas_call(
        kernel,
        out_shape=(pltpu.VMEM((S, KV), F32), pltpu.VMEM((32, DC), F32)),
        in_specs=[hbm] * 9,
        out_specs=(vmem, vmem),
        scratch_shapes=[
            pltpu.VMEM((S, KV), F32),
            pltpu.VMEM((8, S, FR), F32),
            pltpu.VMEM((S, KV), F32),
            pltpu.SMEM((1,), jnp.int32),
            pltpu.SMEM((8,), jnp.int32),
            pltpu.SMEM((8,), jnp.int32),
            pltpu.VMEM((KV, CW), BF16),
            pltpu.VMEM((KV, DC), BF16),
            pltpu.VMEM((32, DC), F32),
            pltpu.VMEM((32, DC), F32),
            pltpu.VMEM((32, S, 256), BF16),
            pltpu.VMEM((32, S, 128), BF16),
            pltpu.VMEM((NZ, S, 128), BF16),
            pltpu.VMEM((NZ, S, 128), BF16),
            pltpu.VMEM((NX, 32, 128), BF16),
            pltpu.VMEM((2, NY, NX, 32, 128), BF16),
            pltpu.VMEM((512, 512), BF16),
            pltpu.VMEM((512, 256), BF16),
            pltpu.VMEM((NV, 32, CW), BF16),
            pltpu.VMEM((NV, 32, CW), BF16),
            pltpu.VMEM((NV, 32, CW), BF16),
            pltpu.VMEM((NV, 32, CW), BF16),
            pltpu.VMEM((NV, 32, CW), F32),
            pltpu.VMEM((NV, 32, CW), F32),
            pltpu.VMEM((NX, 128, 256), BF16),
            pltpu.VMEM((NX, NZ, S, 128), BF16),
            pltpu.VMEM((NX - 1, 128, 256), BF16),
            pltpu.VMEM((NZ - 1, NX, S, 128), BF16),
            pltpu.VMEM((NZ, S, 256), BF16),
            pltpu.VMEM((NX, S, 128), BF16),
            pltpu.VMEM((NZ - 1, S, 256), BF16),
            pltpu.VMEM((NX - 1, S, 128), BF16),
            pltpu.VMEM((NV, S, CW), BF16),
            pltpu.VMEM((NY, S, KV), F32),
            pltpu.SemaphoreType.DMA((10,)),
            pltpu.SemaphoreType.DMA((N_SENT,)),
            pltpu.SemaphoreType.DMA((N_ARRIVED,)),
        ],
        compiler_params=pltpu.CompilerParams(collective_id=0, has_side_effects=True, vmem_limit_bytes=60 << 20),
        cost_estimate=pl.CostEstimate(flops=500_000_000, bytes_accessed=3_000_000, transcendentals=0),
        name="sirt",
    )(
        volume, foot, column_footprint_weights, tile_rows, table_offset, view_angle,
        measured.reshape(32, DC), row_scale.reshape(32, DC), column_scale,
    )
    return pl.pallas_call(
        hand_over,
        out_shape=(jax.ShapeDtypeStruct((S, KV), F32), jax.ShapeDtypeStruct((4, 8, DC), F32)),
        in_specs=[vmem] * 2,
        out_specs=(hbm, hbm),
        scratch_shapes=[pltpu.SemaphoreType.DMA((2,))],
        compiler_params=pltpu.CompilerParams(vmem_limit_bytes=4 << 20),
        name="hand_over",
    )(updated, weighted.reshape(4, 8, DC))


def solution(mesh):
    placed = (
        P(None, "vol"),
        P("view", "vol", None, None),
        P("vol", None),
        P("vol"),
        P("view"),
        P("view"),
        P("vol", "view", None),
        P("vol", "view", None),
        P(None, "vol"),
    )
    return jax.shard_map(
        body,
        mesh=mesh,
        in_specs=placed,
        out_specs=(P(None, "vol"), P("vol", "view", None)),
        check_vma=False,
    )
```

```python
import functools

import jax
import jax.numpy as jnp
from jax import lax
from jax.experimental import pallas as pl
from jax.experimental.pallas import tpu as pltpu
from jax.sharding import PartitionSpec as P

MESH = pl.DeviceIdType.MESH
F32, BF16 = jnp.float32, jnp.bfloat16
S, FR, DR, DC, KV = 16, 80, 128, 3072, 1024
NX, NY, NZ, NV = 4, 4, 8, 8
CW = DC // 8
CHUNKS = ((0, 256), (256, 128))
FAR_Z = (4, 3, 5, 2, 6, 1, 7)
(FZ_S, M_S, R_S, Y1X_S, Y1Z_S, Y0Z_S, Y0X_S, F_S, _, FC_S, Z0X_S, Z1Z_S, Z0Z_S, Z1X_S, P_S, SV_S) = range(16)
(FZ_R, M_R, R_R, Y1Z_R, Y0X_R, FC_R, Z0X_R, Z1Z_R, Z0Z_R, Z1X_R, P_R) = range(11)
Y1X_R, Y0Z_R, F_R, SV_R = 11, 14, 21, 25
N_SENT, N_ARRIVED = 16, 29


def split2(a):
    hi = a.astype(BF16)
    return hi, (a - hi.astype(F32)).astype(BF16)


def barrel(a, shift):
    for bit in range(12):
        moved = pltpu.roll(a, 1 << bit, 1)
        on = jnp.broadcast_to((shift >> bit) & 1, a.shape)
        a = jnp.where(on == 1, moved, a)
    return a


def kernel(
    vol_hbm, foot_hbm, c_hbm, tile_hbm, offset_hbm, angle_hbm, m_hbm, r_hbm, cs_hbm,
    upd_ref, wtd_ref,
    vol_ref, foot_ref, cs_ref, tile_s, offset_s, angle_s, cbuf, cfull, cturned, mraw, rraw, ybuf0, ybuf1, pbuf, gbuf, gt, a4, acat, atb,
    msend, rsend, mrecv, rrecv, psend, precv,
    zsend0, zsend1, zrecv0, zrecv1, ssend0, ssend1, srecv0, srecv1, sall, uall,
    lsem, ssem, rsem,
):
    d = lax.axis_index("vol")
    g = lax.axis_index("view")
    x, z = d // NZ, d % NZ
    y, c = g // 2, g % 2

    def xp(o):
        return (lax.rem(x + o, NX) * NZ + z, g)

    def zp(o):
        return (x * NZ + lax.rem(z + o, NZ), g)

    def vp(o):
        return (d, lax.rem(g + o, NV))

    def yp(o):
        return (d, lax.rem(y + o, NY) * 2 + c)

    def vq(o, swap):
        return (d, lax.rem(y + o, NY) * 2 + (1 - c if swap else c))

    def xyp(p, o):
        return (lax.rem(x + p, NX) * NZ + z, lax.rem(y + o, NY) * 2 + c)

    core = (d, y * 2 + (1 - c))

    def transfer(src, dst, device, s, r):
        return pltpu.make_async_remote_copy(
            src_ref=src, dst_ref=dst, send_sem=ssem.at[s], recv_sem=rsem.at[r], device_id=device, device_id_type=MESH
        )

    def send(src, dst, device, s, r):
        transfer(src, dst, device, s, r).start()

    def arrived(ref, r):
        transfer(ref, ref, core, 0, r).wait_recv()

    def sent(ref, s):
        transfer(ref, ref, core, s, 0).wait_send()

    barrier = pltpu.get_barrier_semaphore()
    partners = [xp(o) for o in range(1, NX)] + [zp(o) for o in range(1, NZ)] + [vp(o) for o in range(1, NV)]
    partners += [xyp(p, o) for p in range(1, NX) for o in range(1, NY)]
    for device in partners:
        pl.semaphore_signal(barrier, inc=1, device_id=device, device_id_type=MESH)

    own_cols = pl.ds(pl.multiple_of(g * CW, 128), CW)
    fetches = [
        pltpu.make_async_copy(src, dst, lsem.at[n])
        for n, (src, dst) in enumerate((
            (tile_hbm, tile_s), (offset_hbm, offset_s), (angle_hbm, angle_s), (foot_hbm, foot_ref),
            (m_hbm, mraw), (r_hbm, rraw), (c_hbm.at[:, own_cols], cbuf), (vol_hbm, vol_ref),
            (cs_hbm, cs_ref), (c_hbm, cfull),
        ))
    ]
    for copy in fetches[:-1]:
        copy.start()
    tile_in, offset_in, angle_in, foot_in, m_in, r_in, c_in, vol_in, cs_in, cfull_in = fetches

    for copy in (tile_in, offset_in, angle_in, foot_in):
        copy.wait()
    view = lax.broadcasted_iota(jnp.int32, (8, 1), 0)
    start = jnp.zeros((8, 1), jnp.int32)
    angle = jnp.zeros((8, 1), jnp.int32)
    for v in range(8):
        start = jnp.where(view == v, tile_s[0] + offset_s[v], start)
        angle = jnp.where(view == v, angle_s[v], angle)
    foot = jnp.concatenate([jnp.pad(foot_ref[v], ((0, 0), (0, 128 - FR))) for v in range(8)], axis=1)
    f_all = jnp.concatenate(split2(foot), axis=0)
    source = lax.broadcasted_iota(jnp.int32, (128, 1024), 1)
    first = jnp.concatenate([start] * 16, axis=0)
    lane = lax.broadcasted_iota(jnp.int32, (128, 1), 0)
    for zz in range(NZ):
        wanted = (lane // 32) * 32 + zz * 4 + (lane % 32) // 8 - first
        wanted = jnp.where((wanted >= 0) & (wanted < FR), wanted + (lane % 8) * 128, -1)
        one_hot = (source == wanted).astype(F32).astype(BF16)
        placed = lax.dot_general(f_all, one_hot, (((1,), (1,)), ((), ())), preferred_element_type=F32)
        placed = placed[:S] + placed[S:]
        pbuf[zz] = (placed * placed).astype(BF16)

    pl.semaphore_wait(barrier, len(partners))

    for o in range(1, NZ):
        send(pbuf.at[lax.rem(z + o, NZ)], gbuf.at[z], zp(o), FZ_S, FZ_R)
    gbuf[z] = pbuf[z]

    vol_in.wait()
    v_all = jnp.concatenate(split2(vol_ref[...]), axis=0)
    c_in.wait()
    prod = jnp.dot(v_all, cbuf[...], preferred_element_type=F32)
    own = (prod[:S] + prod[S:]).astype(BF16)
    ybuf0[d] = own[:, :256]
    ybuf1[d] = own[:, 256:]
    for n, o in enumerate((2, 1, 3)):
        send(ybuf1.at[d], ybuf1.at[d], xp(o), Y1X_S, Y1X_R + n)
    for o in range(1, NZ):
        send(ybuf0.at[d], ybuf0.at[d], zp(o), Y0Z_S, Y0Z_R + o - 1)
    for o in (2, 1, 3):
        send(ybuf0.at[d], ybuf0.at[d], xp(o), Y0X_S, Y0X_R)
    for o in range(1, NZ):
        send(ybuf1.at[d], ybuf1.at[d], zp(o), Y1Z_S, Y1Z_R)

    shift_back = jnp.where(angle == 0, 0, DC - angle)
    for copy_in, raw, out, got, s, r in ((m_in, mraw, msend, mrecv, M_S, M_R), (r_in, rraw, rsend, rrecv, R_S, R_R)):
        copy_in.wait()
        for i in range(0, 4, 2):
            rolled = [barrel(raw[8 * n : 8 * n + 8, :], shift_back) for n in (i, i + 1)]
            rolled = jnp.concatenate(rolled, axis=0).astype(BF16)
            for k in range(NV):
                out[k, 8 * i : 8 * i + 16, :] = rolled[:, k * CW : (k + 1) * CW]
        for o in (4, 3, 5, 2, 6, 1, 7):
            send(out.at[lax.rem(g + o, NV)], got.at[g], vp(o), s, r)
        got[g] = out[g]
    cfull_in.start()

    arrived(gbuf.at[pl.ds(0, NZ - 1)], FZ_R)
    turned = jnp.transpose(gbuf[...].astype(F32).reshape(NZ * S, 128))
    gt[...] = turned.astype(BF16).reshape(NX, 32, 128)
    for p, o in [(p, o) for p in (0, 2, 1, 3) for o in (2, 1, 3, 0) if p or o]:
        send(gt.at[lax.rem(x + p, NX)], a4.at[c, y, x], xyp(p, o), F_S + min(p, 1), F_R + p)
    a4[c, y, x] = gt[x]

    for n, o in enumerate((2, 1, 3)):
        tile = lax.rem(x + NX - o, NX) * NZ + z
        arrived(ybuf1.at[tile], Y1X_R + n)
        for p in range(1, NZ):
            send(ybuf1.at[tile], ybuf1.at[tile], zp(p), Y1Z_S, Y1Z_R)
    for o in range(1, NZ):
        tile = x * NZ + lax.rem(z + NZ - o, NZ)
        arrived(ybuf0.at[tile], Y0Z_R + o - 1)
        for p in (2, 1, 3):
            send(ybuf0.at[tile], ybuf0.at[tile], xp(p), Y0X_S, Y0X_R)

    def turn(block, carry):
        cols = pl.ds(pl.multiple_of(block * 128, 128), 128)
        cturned[cols, :] = jnp.transpose(cfull[:, cols])
        return carry

    cfull_in.wait()
    lax.fori_loop(0, 8, turn, 0)

    for p in (0, 2, 1, 3):
        column = a4.at[c, :, lax.rem(x + NX - p, NX)]
        arrived(column if p else a4.at[c, pl.ds(0, NY - 1), x], F_R + p)
        send(column, column, core, FC_S, FC_R)
    arrived(a4.at[1 - c], FC_R)

    for k in range(NX):
        part = jnp.sqrt(jnp.concatenate([a4[v % 2, v // 2, k] for v in range(NV)], axis=0).astype(F32))
        hi, lo = split2(part)
        acat[0:256, k * 128 : (k + 1) * 128] = hi
        acat[256:512, k * 128 : (k + 1) * 128] = lo
        atb[k * 128 : (k + 1) * 128, :] = jnp.transpose(part).astype(BF16)

    arrived(ybuf0.at[pl.ds(0, NZ * (NX - 1))], Y0X_R)
    arrived(ybuf1.at[pl.ds(0, NX * (NZ - 1))], Y1Z_R)
    arrived(mrecv.at[pl.ds(0, NV - 1)], M_R)
    arrived(rrecv.at[pl.ds(0, NV - 1)], R_R)
    for j, (first, width) in enumerate(CHUNKS):
        cols = pl.ds(first, width)
        proj = jnp.dot(acat[...], (ybuf0, ybuf1)[j][...].reshape(NX * NZ * S, width), preferred_element_type=F32)
        proj = proj[:256] + proj[256:]
        psend[:, :, cols] = proj.reshape(NV, 32, width)
        measured = mrecv[:, :, cols].astype(F32).reshape(256, width)
        weighted = rrecv[:, :, cols].astype(F32).reshape(256, width) * (measured - proj)
        part = jnp.dot(atb[...], weighted.astype(BF16), preferred_element_type=F32)
        part = part.astype(BF16)
        if j == 0:
            zsend0[...] = part.reshape(NX, 128, width)
            for o in (2, 1, 3):
                send(zsend0.at[lax.rem(x + o, NX)], zrecv0.at[o - 1], xp(o), Z0X_S, Z0X_R)
        else:
            zsend1[...] = part.reshape(NX, NZ, S, width)
            for o in FAR_Z:
                send(zsend1.at[:, lax.rem(z + o, NZ)], zrecv1.at[o - 1], zp(o), Z1Z_S, Z1Z_R)

    for o in (1, 7, 2, 6, 3, 5, 4):
        send(psend.at[lax.rem(g + o, NV)], precv.at[g], vp(o), P_S, P_R)
    precv[g] = psend[g]

    lax.fori_loop(8, 18, turn, 0)

    arrived(zrecv0, Z0X_R)
    total = zsend0[x].astype(F32)
    for o in range(NX - 1):
        total += zrecv0[o].astype(F32)
    ssend0[...] = total.astype(BF16).reshape(NZ, S, 256)
    for o in FAR_Z:
        send(ssend0.at[lax.rem(z + o, NZ)], srecv0.at[o - 1], zp(o), Z0Z_S, Z0Z_R)

    arrived(zrecv1, Z1Z_R)
    total = zsend1[:, z].astype(F32)
    for o in range(NZ - 1):
        total += zrecv1[o].astype(F32)
    ssend1[...] = total.astype(BF16)
    for o in (2, 1, 3):
        send(ssend1.at[lax.rem(x + o, NX)], srecv1.at[o - 1], xp(o), Z1X_S, Z1X_R)

    lax.fori_loop(18, DC // 128, turn, 0)

    arrived(srecv0, Z0Z_R)
    total = ssend0[z].astype(F32)
    for o in range(NZ - 1):
        total += srecv0[o].astype(F32)
    sall[g, :, :256] = total.astype(BF16)

    arrived(srecv1, Z1X_R)
    total = ssend1[x].astype(F32)
    for o in range(NX - 1):
        total += srecv1[o].astype(F32)
    sall[g, :, 256:] = total.astype(BF16)

    for o in (2, 1, 3):
        for swap in (False, True):
            send(sall.at[g], sall.at[g], vq(o, swap), SV_S, SV_R + o)
    send(sall.at[g], sall.at[g], core, SV_S, SV_R)

    arrived(precv.at[pl.ds(0, NV - 1)], P_R)
    for i in range(4):
        rows = slice(8 * i, 8 * i + 8)
        row = jnp.concatenate([precv[k, rows, :] for k in range(NV)], axis=1)
        wtd_ref[rows, :] = rraw[rows, :] * (mraw[rows, :] - barrel(row, angle))

    cs_in.wait()
    for o in (0, 1, 3, 2):
        arrived(sall.at[pl.ds(0, 2 if o else 1)], SV_R + o)
        group = lax.rem(y + NY - o, NY)
        both = jnp.concatenate([sall[2 * group], sall[2 * group + 1]], axis=1)
        weights = cturned[pl.ds(pl.multiple_of(group * 2 * CW, 128), 2 * CW), :]
        uall[group] = jnp.dot(both, weights, preferred_element_type=F32)

    total = ((uall[0] + uall[1]) + uall[2]) + uall[3]
    upd_ref[...] = vol_ref[...] + cs_ref[...] * total
    for ref, s in (
        (gbuf.at[pl.ds(0, NZ - 1)], FZ_S), (mrecv.at[pl.ds(0, NV - 1)], M_S), (rrecv.at[pl.ds(0, NV - 1)], R_S),
        (ybuf1.at[pl.ds(0, NX - 1)], Y1X_S), (ybuf1.at[pl.ds(0, NX * (NZ - 1))], Y1Z_S),
        (ybuf0.at[pl.ds(0, NZ - 1)], Y0Z_S), (ybuf0.at[pl.ds(0, NZ * (NX - 1))], Y0X_S),
        (a4.at[0, 0, pl.ds(0, 3)], F_S), (a4.at[0, :, pl.ds(0, 3)], F_S + 1), (a4.at[0], FC_S),
        (zrecv0, Z0X_S), (zrecv1, Z1Z_S), (srecv0, Z0Z_S), (srecv1, Z1X_S),
        (precv.at[pl.ds(0, NV - 1)], P_S), (sall.at[pl.ds(0, NV - 1)], SV_S),
    ):
        sent(ref, s)


def hand_over(upd_in, wtd_in, upd_out, wtd_out, sem):
    copies = (pltpu.make_async_copy(wtd_in, wtd_out, sem.at[0]), pltpu.make_async_copy(upd_in, upd_out, sem.at[1]))
    for copy in copies:
        copy.start()
    for copy in copies:
        copy.wait()


def body(volume, row_footprint, column_footprint_weights, tile_rows, table_offset, view_angle, measured, row_scale, column_scale):
    foot = jnp.transpose(row_footprint[:, 0], (0, 2, 1))
    hbm = pl.BlockSpec(memory_space=pltpu.HBM)
    vmem = pl.BlockSpec(memory_space=pltpu.VMEM)
    updated, weighted = pl.pallas_call(
        kernel,
        out_shape=(pltpu.VMEM((S, KV), F32), pltpu.VMEM((32, DC), F32)),
        in_specs=[hbm] * 9,
        out_specs=(vmem, vmem),
        scratch_shapes=[
            pltpu.VMEM((S, KV), F32),
            pltpu.VMEM((8, S, FR), F32),
            pltpu.VMEM((S, KV), F32),
            pltpu.SMEM((1,), jnp.int32),
            pltpu.SMEM((8,), jnp.int32),
            pltpu.SMEM((8,), jnp.int32),
            pltpu.VMEM((KV, CW), BF16),
            pltpu.VMEM((KV, DC), BF16),
            pltpu.VMEM((DC, KV), BF16),
            pltpu.VMEM((32, DC), F32),
            pltpu.VMEM((32, DC), F32),
            pltpu.VMEM((32, S, 256), BF16),
            pltpu.VMEM((32, S, 128), BF16),
            pltpu.VMEM((NZ, S, 128), BF16),
            pltpu.VMEM((NZ, S, 128), BF16),
            pltpu.VMEM((NX, 32, 128), BF16),
            pltpu.VMEM((2, NY, NX, 32, 128), BF16),
            pltpu.VMEM((512, 512), BF16),
            pltpu.VMEM((512, 256), BF16),
            pltpu.VMEM((NV, 32, CW), BF16),
            pltpu.VMEM((NV, 32, CW), BF16),
            pltpu.VMEM((NV, 32, CW), BF16),
            pltpu.VMEM((NV, 32, CW), BF16),
            pltpu.VMEM((NV, 32, CW), F32),
            pltpu.VMEM((NV, 32, CW), F32),
            pltpu.VMEM((NX, 128, 256), BF16),
            pltpu.VMEM((NX, NZ, S, 128), BF16),
            pltpu.VMEM((NX - 1, 128, 256), BF16),
            pltpu.VMEM((NZ - 1, NX, S, 128), BF16),
            pltpu.VMEM((NZ, S, 256), BF16),
            pltpu.VMEM((NX, S, 128), BF16),
            pltpu.VMEM((NZ - 1, S, 256), BF16),
            pltpu.VMEM((NX - 1, S, 128), BF16),
            pltpu.VMEM((NV, S, CW), BF16),
            pltpu.VMEM((NY, S, KV), F32),
            pltpu.SemaphoreType.DMA((10,)),
            pltpu.SemaphoreType.DMA((N_SENT,)),
            pltpu.SemaphoreType.DMA((N_ARRIVED,)),
        ],
        compiler_params=pltpu.CompilerParams(collective_id=0, has_side_effects=True, vmem_limit_bytes=60 << 20),
        cost_estimate=pl.CostEstimate(flops=500_000_000, bytes_accessed=3_000_000, transcendentals=0),
        name="sirt",
    )(
        volume, foot, column_footprint_weights, tile_rows, table_offset, view_angle,
        measured.reshape(32, DC), row_scale.reshape(32, DC), column_scale,
    )
    return pl.pallas_call(
        hand_over,
        out_shape=(jax.ShapeDtypeStruct((S, KV), F32), jax.ShapeDtypeStruct((4, 8, DC), F32)),
        in_specs=[vmem] * 2,
        out_specs=(hbm, hbm),
        scratch_shapes=[pltpu.SemaphoreType.DMA((2,))],
        compiler_params=pltpu.CompilerParams(vmem_limit_bytes=4 << 20),
        name="hand_over",
    )(updated, weighted.reshape(4, 8, DC))


def solution(mesh):
    placed = (
        P(None, "vol"),
        P("view", "vol", None, None),
        P("vol", None),
        P("vol"),
        P("view"),
        P("view"),
        P("vol", "view", None),
        P("vol", "view", None),
        P(None, "vol"),
    )
    return jax.shard_map(
        body,
        mesh=mesh,
        in_specs=placed,
        out_specs=(P(None, "vol"), P("vol", "view", None)),
        check_vma=False,
    )
```

```python
import functools

import jax
import jax.numpy as jnp
from jax import lax
from jax.experimental import pallas as pl
from jax.experimental.pallas import tpu as pltpu
from jax.sharding import PartitionSpec as P

MESH = pl.DeviceIdType.MESH
F32, BF16 = jnp.float32, jnp.bfloat16
S, FR, DR, DC, KV = 16, 80, 128, 3072, 1024
NX, NY, NZ, NV = 4, 4, 8, 8
CW = DC // 8
CHUNKS = ((0, 128), (128, 128), (256, 128))
FAR_Z = (4, 3, 5, 2, 6, 1, 7)
(FZ_S, M_S, R_S, Y1X_S, Y1Z_S, Y0Z_S, Y0X_S, F_S, _, FC_S, Z0X_S, Z1Z_S, Z0Z_S, Z1X_S, P_S, SV_S) = range(16)
(FZ_R, M_R, R_R, Y1Z_R, Y0X_R, FC_R, Z0X_R, Z1Z_R, Z0Z_R, Z1X_R, P_R) = range(11)
Y1X_R, Y0Z_R, F_R, SV_R, Z0XB_R, Z0ZB_R = 11, 14, 21, 25, 29, 30
N_SENT, N_ARRIVED = 16, 31


def split2(a):
    hi = a.astype(BF16)
    return hi, (a - hi.astype(F32)).astype(BF16)


def barrel(a, shift):
    for bit in range(12):
        moved = pltpu.roll(a, 1 << bit, 1)
        on = jnp.broadcast_to((shift >> bit) & 1, a.shape)
        a = jnp.where(on == 1, moved, a)
    return a


def kernel(
    vol_hbm, foot_hbm, c_hbm, tile_hbm, offset_hbm, angle_hbm, m_hbm, r_hbm, cs_hbm,
    upd_ref, wtd_ref,
    vol_ref, foot_ref, cs_ref, tile_s, offset_s, angle_s, cbuf, cfull, cturned, mraw, rraw, ybuf0, ybuf1, pbuf, gbuf, gt, a4, acat, atb,
    msend, rsend, mrecv, rrecv, psend, precv,
    zsend0, zsend1, zrecv0, zrecv1, ssend0, ssend1, srecv0, srecv1, sall, uall,
    lsem, ssem, rsem,
):
    d = lax.axis_index("vol")
    g = lax.axis_index("view")
    x, z = d // NZ, d % NZ
    y, c = g // 2, g % 2

    def xp(o):
        return (lax.rem(x + o, NX) * NZ + z, g)

    def zp(o):
        return (x * NZ + lax.rem(z + o, NZ), g)

    def vp(o):
        return (d, lax.rem(g + o, NV))

    def yp(o):
        return (d, lax.rem(y + o, NY) * 2 + c)

    def vq(o, swap):
        return (d, lax.rem(y + o, NY) * 2 + (1 - c if swap else c))

    def xyp(p, o):
        return (lax.rem(x + p, NX) * NZ + z, lax.rem(y + o, NY) * 2 + c)

    core = (d, y * 2 + (1 - c))

    def transfer(src, dst, device, s, r):
        return pltpu.make_async_remote_copy(
            src_ref=src, dst_ref=dst, send_sem=ssem.at[s], recv_sem=rsem.at[r], device_id=device, device_id_type=MESH
        )

    def send(src, dst, device, s, r):
        transfer(src, dst, device, s, r).start()

    def arrived(ref, r):
        transfer(ref, ref, core, 0, r).wait_recv()

    def sent(ref, s):
        transfer(ref, ref, core, s, 0).wait_send()

    barrier = pltpu.get_barrier_semaphore()
    partners = [xp(o) for o in range(1, NX)] + [zp(o) for o in range(1, NZ)] + [vp(o) for o in range(1, NV)]
    partners += [xyp(p, o) for p in range(1, NX) for o in range(1, NY)]
    for device in partners:
        pl.semaphore_signal(barrier, inc=1, device_id=device, device_id_type=MESH)

    own_cols = pl.ds(pl.multiple_of(g * CW, 128), CW)
    fetches = [
        pltpu.make_async_copy(src, dst, lsem.at[n])
        for n, (src, dst) in enumerate((
            (tile_hbm, tile_s), (offset_hbm, offset_s), (angle_hbm, angle_s), (foot_hbm, foot_ref),
            (m_hbm, mraw), (r_hbm, rraw), (c_hbm.at[:, own_cols], cbuf), (vol_hbm, vol_ref),
            (cs_hbm, cs_ref), (c_hbm, cfull),
        ))
    ]
    for copy in fetches[:-1]:
        copy.start()
    tile_in, offset_in, angle_in, foot_in, m_in, r_in, c_in, vol_in, cs_in, cfull_in = fetches

    for copy in (tile_in, offset_in, angle_in, foot_in):
        copy.wait()
    view = lax.broadcasted_iota(jnp.int32, (8, 1), 0)
    start = jnp.zeros((8, 1), jnp.int32)
    angle = jnp.zeros((8, 1), jnp.int32)
    for v in range(8):
        start = jnp.where(view == v, tile_s[0] + offset_s[v], start)
        angle = jnp.where(view == v, angle_s[v], angle)
    foot = jnp.concatenate([jnp.pad(foot_ref[v], ((0, 0), (0, 128 - FR))) for v in range(8)], axis=1)
    f_all = jnp.concatenate(split2(foot), axis=0)
    source = lax.broadcasted_iota(jnp.int32, (128, 1024), 1)
    first = jnp.concatenate([start] * 16, axis=0)
    lane = lax.broadcasted_iota(jnp.int32, (128, 1), 0)
    for zz in range(NZ):
        wanted = (lane // 32) * 32 + zz * 4 + (lane % 32) // 8 - first
        wanted = jnp.where((wanted >= 0) & (wanted < FR), wanted + (lane % 8) * 128, -1)
        one_hot = (source == wanted).astype(F32).astype(BF16)
        placed = lax.dot_general(f_all, one_hot, (((1,), (1,)), ((), ())), preferred_element_type=F32)
        placed = placed[:S] + placed[S:]
        pbuf[zz] = (placed * placed).astype(BF16)

    pl.semaphore_wait(barrier, len(partners))

    for o in range(1, NZ):
        send(pbuf.at[lax.rem(z + o, NZ)], gbuf.at[z], zp(o), FZ_S, FZ_R)
    gbuf[z] = pbuf[z]

    vol_in.wait()
    v_all = jnp.concatenate(split2(vol_ref[...]), axis=0)
    c_in.wait()
    prod = jnp.dot(v_all, cbuf[...], preferred_element_type=F32)
    own = (prod[:S] + prod[S:]).astype(BF16)
    ybuf0[d] = own[:, :256]
    ybuf1[d] = own[:, 256:]
    for n, o in enumerate((2, 1, 3)):
        send(ybuf1.at[d], ybuf1.at[d], xp(o), Y1X_S, Y1X_R + n)
    for o in range(1, NZ):
        send(ybuf0.at[d], ybuf0.at[d], zp(o), Y0Z_S, Y0Z_R + o - 1)
    for o in (2, 1, 3):
        send(ybuf0.at[d], ybuf0.at[d], xp(o), Y0X_S, Y0X_R)
    for o in range(1, NZ):
        send(ybuf1.at[d], ybuf1.at[d], zp(o), Y1Z_S, Y1Z_R)

    shift_back = jnp.where(angle == 0, 0, DC - angle)
    for copy_in, raw, out, got, s, r in ((m_in, mraw, msend, mrecv, M_S, M_R), (r_in, rraw, rsend, rrecv, R_S, R_R)):
        copy_in.wait()
        for i in range(0, 4, 2):
            rolled = [barrel(raw[8 * n : 8 * n + 8, :], shift_back) for n in (i, i + 1)]
            rolled = jnp.concatenate(rolled, axis=0).astype(BF16)
            for k in range(NV):
                out[k, 8 * i : 8 * i + 16, :] = rolled[:, k * CW : (k + 1) * CW]
        for o in (4, 3, 5, 2, 6, 1, 7):
            send(out.at[lax.rem(g + o, NV)], got.at[g], vp(o), s, r)
        got[g] = out[g]
    cfull_in.start()

    arrived(gbuf.at[pl.ds(0, NZ - 1)], FZ_R)
    turned = jnp.transpose(gbuf[...].astype(F32).reshape(NZ * S, 128))
    gt[...] = turned.astype(BF16).reshape(NX, 32, 128)
    for p, o in [(p, o) for p in (0, 2, 1, 3) for o in (2, 1, 3, 0) if p or o]:
        send(gt.at[lax.rem(x + p, NX)], a4.at[c, y, x], xyp(p, o), F_S + min(p, 1), F_R + p)
    a4[c, y, x] = gt[x]

    for n, o in enumerate((2, 1, 3)):
        tile = lax.rem(x + NX - o, NX) * NZ + z
        arrived(ybuf1.at[tile], Y1X_R + n)
        for p in range(1, NZ):
            send(ybuf1.at[tile], ybuf1.at[tile], zp(p), Y1Z_S, Y1Z_R)
    for o in range(1, NZ):
        tile = x * NZ + lax.rem(z + NZ - o, NZ)
        arrived(ybuf0.at[tile], Y0Z_R + o - 1)
        for p in (2, 1, 3):
            send(ybuf0.at[tile], ybuf0.at[tile], xp(p), Y0X_S, Y0X_R)

    def turn(block, carry):
        cols = pl.ds(pl.multiple_of(block * 128, 128), 128)
        cturned[cols, :] = jnp.transpose(cfull[:, cols])
        return carry

    cfull_in.wait()
    lax.fori_loop(0, 8, turn, 0)

    for p in (0, 2, 1, 3):
        column = a4.at[c, :, lax.rem(x + NX - p, NX)]
        arrived(column if p else a4.at[c, pl.ds(0, NY - 1), x], F_R + p)
        send(column, column, core, FC_S, FC_R)
    arrived(a4.at[1 - c], FC_R)

    for k in range(NX):
        part = jnp.sqrt(jnp.concatenate([a4[v % 2, v // 2, k] for v in range(NV)], axis=0).astype(F32))
        hi, lo = split2(part)
        acat[0:256, k * 128 : (k + 1) * 128] = hi
        acat[256:512, k * 128 : (k + 1) * 128] = lo
        atb[k * 128 : (k + 1) * 128, :] = jnp.transpose(part).astype(BF16)

    arrived(ybuf0.at[pl.ds(0, NZ * (NX - 1))], Y0X_R)
    arrived(ybuf1.at[pl.ds(0, NX * (NZ - 1))], Y1Z_R)
    arrived(mrecv.at[pl.ds(0, NV - 1)], M_R)
    arrived(rrecv.at[pl.ds(0, NV - 1)], R_R)
    for j, (first, width) in enumerate(CHUNKS):
        cols = pl.ds(first, width)
        proj = jnp.dot(acat[...], (ybuf1[...] if j == 2 else ybuf0[:, :, cols]).reshape(NX * NZ * S, width), preferred_element_type=F32)
        proj = proj[:256] + proj[256:]
        psend[:, :, cols] = proj.reshape(NV, 32, width)
        measured = mrecv[:, :, cols].astype(F32).reshape(256, width)
        weighted = rrecv[:, :, cols].astype(F32).reshape(256, width) * (measured - proj)
        part = jnp.dot(atb[...], weighted.astype(BF16), preferred_element_type=F32)
        part = part.astype(BF16)
        if j < 2:
            zsend0[j] = part.reshape(NX, 128, width)
            for o in (2, 1, 3):
                send(zsend0.at[j, lax.rem(x + o, NX)], zrecv0.at[j, o - 1], xp(o), Z0X_S, (Z0X_R, Z0XB_R)[j])
        else:
            zsend1[...] = part.reshape(NX, NZ, S, width)
            for o in FAR_Z:
                send(zsend1.at[:, lax.rem(z + o, NZ)], zrecv1.at[o - 1], zp(o), Z1Z_S, Z1Z_R)

    for o in (1, 7, 2, 6, 3, 5, 4):
        send(psend.at[lax.rem(g + o, NV)], precv.at[g], vp(o), P_S, P_R)
    precv[g] = psend[g]

    lax.fori_loop(8, 18, turn, 0)

    for j in range(2):
        arrived(zrecv0.at[j], (Z0X_R, Z0XB_R)[j])
        total = zsend0[j, x].astype(F32)
        for o in range(NX - 1):
            total += zrecv0[j, o].astype(F32)
        ssend0[j] = total.astype(BF16).reshape(NZ, S, 128)
        for o in FAR_Z:
            send(ssend0.at[j, lax.rem(z + o, NZ)], srecv0.at[j, o - 1], zp(o), Z0Z_S, (Z0Z_R, Z0ZB_R)[j])

    arrived(zrecv1, Z1Z_R)
    total = zsend1[:, z].astype(F32)
    for o in range(NZ - 1):
        total += zrecv1[o].astype(F32)
    ssend1[...] = total.astype(BF16)
    for o in (2, 1, 3):
        send(ssend1.at[lax.rem(x + o, NX)], srecv1.at[o - 1], xp(o), Z1X_S, Z1X_R)

    lax.fori_loop(18, DC // 128, turn, 0)

    for j in range(2):
        arrived(srecv0.at[j], (Z0Z_R, Z0ZB_R)[j])
        total = ssend0[j, z].astype(F32)
        for o in range(NZ - 1):
            total += srecv0[j, o].astype(F32)
        sall[g, :, j * 128 : (j + 1) * 128] = total.astype(BF16)

    arrived(srecv1, Z1X_R)
    total = ssend1[x].astype(F32)
    for o in range(NX - 1):
        total += srecv1[o].astype(F32)
    sall[g, :, 256:] = total.astype(BF16)

    for o in (2, 1, 3):
        for swap in (False, True):
            send(sall.at[g], sall.at[g], vq(o, swap), SV_S, SV_R + o)
    send(sall.at[g], sall.at[g], core, SV_S, SV_R)

    arrived(precv.at[pl.ds(0, NV - 1)], P_R)
    for i in range(4):
        rows = slice(8 * i, 8 * i + 8)
        row = jnp.concatenate([precv[k, rows, :] for k in range(NV)], axis=1)
        wtd_ref[rows, :] = rraw[rows, :] * (mraw[rows, :] - barrel(row, angle))

    cs_in.wait()
    for o in (0, 1, 3, 2):
        arrived(sall.at[pl.ds(0, 2 if o else 1)], SV_R + o)
        group = lax.rem(y + NY - o, NY)
        both = jnp.concatenate([sall[2 * group], sall[2 * group + 1]], axis=1)
        weights = cturned[pl.ds(pl.multiple_of(group * 2 * CW, 128), 2 * CW), :]
        uall[group] = jnp.dot(both, weights, preferred_element_type=F32)

    total = ((uall[0] + uall[1]) + uall[2]) + uall[3]
    upd_ref[...] = vol_ref[...] + cs_ref[...] * total
    for ref, s in (
        (gbuf.at[pl.ds(0, NZ - 1)], FZ_S), (mrecv.at[pl.ds(0, NV - 1)], M_S), (rrecv.at[pl.ds(0, NV - 1)], R_S),
        (ybuf1.at[pl.ds(0, NX - 1)], Y1X_S), (ybuf1.at[pl.ds(0, NX * (NZ - 1))], Y1Z_S),
        (ybuf0.at[pl.ds(0, NZ - 1)], Y0Z_S), (ybuf0.at[pl.ds(0, NZ * (NX - 1))], Y0X_S),
        (a4.at[0, 0, pl.ds(0, 3)], F_S), (a4.at[0, :, pl.ds(0, 3)], F_S + 1), (a4.at[0], FC_S),
        (zrecv0, Z0X_S), (zrecv1, Z1Z_S), (srecv0, Z0Z_S), (srecv1, Z1X_S),
        (precv.at[pl.ds(0, NV - 1)], P_S), (sall.at[pl.ds(0, NV - 1)], SV_S),
    ):
        sent(ref, s)


def hand_over(upd_in, wtd_in, upd_out, wtd_out, sem):
    copies = (pltpu.make_async_copy(wtd_in, wtd_out, sem.at[0]), pltpu.make_async_copy(upd_in, upd_out, sem.at[1]))
    for copy in copies:
        copy.start()
    for copy in copies:
        copy.wait()


def body(volume, row_footprint, column_footprint_weights, tile_rows, table_offset, view_angle, measured, row_scale, column_scale):
    foot = jnp.transpose(row_footprint[:, 0], (0, 2, 1))
    hbm = pl.BlockSpec(memory_space=pltpu.HBM)
    vmem = pl.BlockSpec(memory_space=pltpu.VMEM)
    updated, weighted = pl.pallas_call(
        kernel,
        out_shape=(pltpu.VMEM((S, KV), F32), pltpu.VMEM((32, DC), F32)),
        in_specs=[hbm] * 9,
        out_specs=(vmem, vmem),
        scratch_shapes=[
            pltpu.VMEM((S, KV), F32),
            pltpu.VMEM((8, S, FR), F32),
            pltpu.VMEM((S, KV), F32),
            pltpu.SMEM((1,), jnp.int32),
            pltpu.SMEM((8,), jnp.int32),
            pltpu.SMEM((8,), jnp.int32),
            pltpu.VMEM((KV, CW), BF16),
            pltpu.VMEM((KV, DC), BF16),
            pltpu.VMEM((DC, KV), BF16),
            pltpu.VMEM((32, DC), F32),
            pltpu.VMEM((32, DC), F32),
            pltpu.VMEM((32, S, 256), BF16),
            pltpu.VMEM((32, S, 128), BF16),
            pltpu.VMEM((NZ, S, 128), BF16),
            pltpu.VMEM((NZ, S, 128), BF16),
            pltpu.VMEM((NX, 32, 128), BF16),
            pltpu.VMEM((2, NY, NX, 32, 128), BF16),
            pltpu.VMEM((512, 512), BF16),
            pltpu.VMEM((512, 256), BF16),
            pltpu.VMEM((NV, 32, CW), BF16),
            pltpu.VMEM((NV, 32, CW), BF16),
            pltpu.VMEM((NV, 32, CW), BF16),
            pltpu.VMEM((NV, 32, CW), BF16),
            pltpu.VMEM((NV, 32, CW), F32),
            pltpu.VMEM((NV, 32, CW), F32),
            pltpu.VMEM((2, NX, 128, 128), BF16),
            pltpu.VMEM((NX, NZ, S, 128), BF16),
            pltpu.VMEM((2, NX - 1, 128, 128), BF16),
            pltpu.VMEM((NZ - 1, NX, S, 128), BF16),
            pltpu.VMEM((2, NZ, S, 128), BF16),
            pltpu.VMEM((NX, S, 128), BF16),
            pltpu.VMEM((2, NZ - 1, S, 128), BF16),
            pltpu.VMEM((NX - 1, S, 128), BF16),
            pltpu.VMEM((NV, S, CW), BF16),
            pltpu.VMEM((NY, S, KV), F32),
            pltpu.SemaphoreType.DMA((10,)),
            pltpu.SemaphoreType.DMA((N_SENT,)),
            pltpu.SemaphoreType.DMA((N_ARRIVED,)),
        ],
        compiler_params=pltpu.CompilerParams(collective_id=0, has_side_effects=True, vmem_limit_bytes=60 << 20),
        cost_estimate=pl.CostEstimate(flops=500_000_000, bytes_accessed=3_000_000, transcendentals=0),
        name="sirt",
    )(
        volume, foot, column_footprint_weights, tile_rows, table_offset, view_angle,
        measured.reshape(32, DC), row_scale.reshape(32, DC), column_scale,
    )
    return pl.pallas_call(
        hand_over,
        out_shape=(jax.ShapeDtypeStruct((S, KV), F32), jax.ShapeDtypeStruct((4, 8, DC), F32)),
        in_specs=[vmem] * 2,
        out_specs=(hbm, hbm),
        scratch_shapes=[pltpu.SemaphoreType.DMA((2,))],
        compiler_params=pltpu.CompilerParams(vmem_limit_bytes=4 << 20),
        name="hand_over",
    )(updated, weighted.reshape(4, 8, DC))


def solution(mesh):
    placed = (
        P(None, "vol"),
        P("view", "vol", None, None),
        P("vol", None),
        P("vol"),
        P("view"),
        P("view"),
        P("vol", "view", None),
        P("vol", "view", None),
        P(None, "vol"),
    )
    return jax.shard_map(
        body,
        mesh=mesh,
        in_specs=placed,
        out_specs=(P(None, "vol"), P("vol", "view", None)),
        check_vma=False,
    )
```
